512 devices in a mesh: dp: 64 (over z, y), mp: 8 (over x, core).
Axes of the slice: x: 4, y: 4, z: 16, core: 2. Of those that a mesh axis runs over, the one named last changes fastest.
Arguments:
- gradient: bfloat16 [4096, 16384], P('dp', 'mp')
- second_moment: float32 [4096, 16384], P('dp', 'mp'), may hold values from 0.001 to 0.1
- owner_table: int32 [256], replicated, may hold values from 0 to 63, as said below
- left_stats: float32 [64, 4, 512, 512], P('dp', None, 'mp'), as said below
- right_stats: float32 [64, 4, 512, 512], P('dp', None, 'mp'), as said below
- left_root: bfloat16 [64, 4, 512, 512], P('dp', None, 'mp'), as said below
- right_root: bfloat16 [64, 4, 512, 512], P('dp', None, 'mp'), as said below
- momentum: bfloat16 [64, 4, 512, 512], P('dp', None, 'mp'), may hold values from -12 to 12
Outputs:
- update: bfloat16 [4096, 16384], P('dp', 'mp')
- new_second_moment: float32 [4096, 16384], P('dp', 'mp')
- new_left_stats: float32 [64, 4, 512, 512], P('dp', None, 'mp')
- new_right_stats: float32 [64, 4, 512, 512], P('dp', None, 'mp')
- new_momentum: bfloat16 [64, 4, 512, 512], P('dp', None, 'mp')
The draws below stay inside these ranges and needn't reach their ends.
Inputs may be any that keep to these rules, and one draw needn't show every extreme that they name: `owner_table`: every index of dp owns exactly 4 blocks. Within one band of 32 blocks (block ids b with equal b // 32) no index owns more than 1 block, so the 32 blocks of a band have 32 distinct owners. `left_stats`: symmetric in its last two dimensions. `right_stats`: symmetric in its last two dimensions. `left_root`: symmetric in its last two dimensions. `right_root`: symmetric in its last two dimensions.
All inputs are finite; a program needn't handle non-finite values.
Results may differ from the reference program's by a relative error of at most 0.0095.
Values may be sent and summed in bfloat16 or wider, within the bound.
No kernel may reach another device: no remote copies, remote signals or barrier semaphores. Data moves between devices by JAX's collectives and lax.ppermute only.
A program may use at most 64 MiB of HBM per device.

```python
import math
import jax
import jax.numpy as jnp
from jax import lax

BLK = 512
ROWS = 4096
COLS = 16384
RB = 8
CB = 32
NBLK = 256
OWNERS = 64
BLK_OWN = 4


def symmetric_blocks(key, low_end, high_end, off_scale):
    key_noise, key_diag = jax.random.split(key)
    entries = jax.random.normal(key_noise, (OWNERS, BLK_OWN, BLK, BLK), jnp.float32)
    mixed = (entries + jnp.swapaxes(entries, -1, -2)) * (off_scale / math.sqrt(2.0))
    diagonal = jax.random.uniform(key_diag, (OWNERS, BLK_OWN, BLK), jnp.float32, low_end, high_end)
    identity = jnp.eye(BLK, dtype=jnp.float32)
    return mixed * (1.0 - identity) + identity * diagonal[..., None]


def draw_gradient(key, part):
    key = jax.random.fold_in(key, 11)
    key_rows, key_cols, key_main = jax.random.split(key, 3)
    row_index = jnp.arange(ROWS, dtype=jnp.float32)
    rising = 1.0 + 2.0 * row_index / ROWS
    row_scale = rising * 10.0 ** jax.random.uniform(key_rows, (ROWS,), jnp.float32, -0.5, 0.5)
    col_scale = 10.0 ** jax.random.uniform(key_cols, (COLS,), jnp.float32, -0.5, 0.5)
    entries = jax.random.normal(key_main, (ROWS, COLS), jnp.float32)
    return (0.044 * row_scale[:, None] * col_scale[None, :] * entries).astype(jnp.bfloat16)


def draw_owner_table(key, part):
    key = jax.random.fold_in(key, 5)
    key_owner, key_band, key_shuffle = jax.random.split(key, 3)
    owner_perm = jax.random.permutation(key_owner, OWNERS).astype(jnp.int32)
    band_perm = jax.random.permutation(key_band, RB).astype(jnp.int32)
    shuffles = jax.vmap(lambda single: jax.random.permutation(single, CB))(jax.random.split(key_shuffle, RB)).astype(jnp.int32)
    position = (band_perm[:, None] * CB + shuffles) % OWNERS
    return owner_perm[position].reshape(RB * CB).astype(jnp.int32)


def draw_left_stats(key, part):
    key = jax.random.fold_in(key, 21)
    return symmetric_blocks(key, 1.0, 2.0, 0.5 / math.sqrt(BLK))


def draw_right_stats(key, part):
    key = jax.random.fold_in(key, 31)
    return symmetric_blocks(key, 1.0, 2.0, 0.5 / math.sqrt(BLK))


def draw_left_root(key, part):
    key = jax.random.fold_in(key, 41)
    return symmetric_blocks(key, 0.8, 1.2, 0.5 / math.sqrt(BLK)).astype(jnp.bfloat16)


def draw_right_root(key, part):
    key = jax.random.fold_in(key, 51)
    return symmetric_blocks(key, 0.8, 1.2, 0.5 / math.sqrt(BLK)).astype(jnp.bfloat16)


def levels(own_key, extent, pieces, low, largest):
    factor_of, own = 1.0, jax.random.fold_in(own_key, 6)
    for dim, parts in pieces:
        heights = jnp.exp(jax.random.uniform(jax.random.fold_in(own, dim), (parts,), jnp.float32, low / len(pieces), largest / len(pieces)))
        factor_of = factor_of * jnp.repeat(heights, extent[dim] // parts).reshape([-1 if axis == dim else 1 for axis in range(len(extent))])
    return factor_of


def centred(own_key, shape, scale, most, cuts=(), kind=jnp.bfloat16):
    result = scale * jax.random.normal(own_key, shape, jnp.float32)
    if cuts:
        result = result * levels(own_key, shape, cuts, -0.22, 0.18)
    return jnp.clip(result, -most, most).astype(kind)


def setup_inputs(seed: int = 0) -> dict:
    streams_of = jax.random.split(jax.random.key(seed), 9)
    gradient = draw_gradient(jax.random.fold_in(streams_of[8], 71), 0)
    second_moment = jnp.clip(jnp.exp(math.log(0.1) - 4.6051702 * jax.random.uniform(streams_of[1], (ROWS, COLS), jnp.float32) ** levels(streams_of[1], (ROWS, COLS), ((0, 64), (1, 8)), -0.2, 0.2)), 0.001, 0.1)
    owner_table = draw_owner_table(jax.random.fold_in(streams_of[8], 71), 0)
    left_stats = draw_left_stats(jax.random.fold_in(streams_of[8], 71), 0)
    right_stats = draw_right_stats(jax.random.fold_in(streams_of[8], 71), 0)
    left_root = draw_left_root(jax.random.fold_in(streams_of[8], 71), 0)
    right_root = draw_right_root(jax.random.fold_in(streams_of[8], 71), 0)
    momentum = centred(streams_of[7], (OWNERS, BLK_OWN, BLK, BLK), 2.0, 12.0, ((0, 64), (2, 8)))
    return dict(gradient=gradient, second_moment=second_moment, owner_table=owner_table, left_stats=left_stats, right_stats=right_stats, left_root=left_root, right_root=right_root, momentum=momentum)


def flatten_blocks(array):
    return array.reshape(NBLK, BLK, BLK)

def reference(gradient, second_moment, owner_table, left_stats, right_stats, left_root, right_root, momentum):
    grad_f32 = gradient.astype(jnp.float32)
    new_second_moment = 0.999 * second_moment + 0.001 * grad_f32 * grad_f32
    adam_dir = grad_f32 / (jnp.sqrt(new_second_moment) + 1e-08)
    adam_sq = lax.optimization_barrier(jnp.mean((adam_dir * adam_dir).reshape(RB, BLK, CB, BLK), axis=(1, 3))).reshape(NBLK)
    blocks = gradient.reshape(RB, BLK, CB, BLK).transpose(0, 2, 1, 3).reshape(NBLK, BLK, BLK)
    owned = jnp.argsort(owner_table, stable=True).astype(jnp.int32)

    def per_block(slot_items):
        block_id, left_old, right_old, left_inv, right_inv, moment_old = slot_items
        block = lax.dynamic_index_in_dim(blocks, block_id, 0, keepdims=False)
        left_new = 0.95 * left_old + 0.05 * jnp.dot(block, block.T, preferred_element_type=jnp.float32)
        right_new = 0.95 * right_old + 0.05 * jnp.dot(block.T, block, preferred_element_type=jnp.float32)
        left_applied = jnp.dot(left_inv, block, preferred_element_type=jnp.float32).astype(jnp.bfloat16)
        precond = jnp.dot(left_applied, right_inv, preferred_element_type=jnp.float32)
        adam_part = lax.dynamic_index_in_dim(adam_sq, block_id, 0, keepdims=False)
        graft = jnp.sqrt(adam_part) / jnp.sqrt(jnp.mean(precond * precond) + 1e-06)
        momentum_f = 0.9 * moment_old.astype(jnp.float32) + graft * precond
        return (left_new, right_new, momentum_f)
    left_new, right_new, momentum_f = lax.map(per_block, (owned, flatten_blocks(left_stats), flatten_blocks(right_stats), flatten_blocks(left_root), flatten_blocks(right_root), flatten_blocks(momentum)))
    total_sq = jnp.sum(momentum_f * momentum_f)
    clip_factor = jnp.minimum(1.0, 0.5 * math.sqrt(ROWS * COLS) / jnp.sqrt(total_sq))
    update_blocks = (clip_factor * momentum_f).astype(jnp.bfloat16)
    inverse = jnp.zeros((NBLK,), jnp.int32).at[owned].set(jnp.arange(NBLK, dtype=jnp.int32))
    by_block = update_blocks[inverse]
    update = by_block.reshape(RB, CB, BLK, BLK).transpose(0, 2, 1, 3).reshape(ROWS, COLS)
    owner_shape = (OWNERS, BLK_OWN, BLK, BLK)
    return (update, new_second_moment, left_new.reshape(owner_shape), right_new.reshape(owner_shape), momentum_f.astype(jnp.bfloat16).reshape(owner_shape))
```

```python
import math

import jax
import jax.numpy as jnp
from jax import lax
from jax.experimental import pallas as pl
from jax.experimental.pallas import tpu as pltpu
from jax.sharding import Mesh
from jax.sharding import PartitionSpec as P

BLK = 512
ROWS = 4096
COLS = 16384
YDIM = 4
AXES = ("z", "y", "m")

ZD, MD = 16, 8
OWNERS = ZD * YDIM
BANDS = ROWS // BLK
CB = COLS // BLK
ZZ = ZD // BANDS
SUB = 8
ROW_DEV = 64
LOCAL = COLS // MD
LB = LOCAL // BLK
LANES = 128
TB = BLK // LANES
SLOTS = 4
AREA = BLK * BLK
INV, BAND, OUT, IN, OTHER = 0, 64, 96, 104, 112
PLAN = 128

BF16, F32 = jnp.bfloat16, jnp.float32


def struct(*shape, dtype=BF16):
    return jax.ShapeDtypeStruct(shape, dtype)


def call(body, specs, outs, args, scratch=(), vmem=16, flops=0, name=None):
    space = {"v": pltpu.VMEM, "s": pltpu.SMEM, "a": pl.ANY}
    size = sum(o.size * o.dtype.itemsize for o in outs)
    size += sum(a.size * a.dtype.itemsize for a, k in zip(args, specs) if k == "v")
    return pl.pallas_call(
        body,
        out_shape=tuple(outs),
        in_specs=[pl.BlockSpec(memory_space=space[k]) for k in specs],
        out_specs=tuple(pl.BlockSpec(memory_space=pltpu.VMEM) for _ in outs),
        scratch_shapes=list(scratch),
        compiler_params=pltpu.CompilerParams(vmem_limit_bytes=vmem * 1024 * 1024),
        cost_estimate=pl.CostEstimate(flops=flops, bytes_accessed=size, transcendentals=0),
        name=name,
    )(*args)


def encode(value):
    value = jnp.broadcast_to(value, (SUB, LANES))
    row = lax.broadcasted_iota(jnp.int32, (SUB, LANES), 0)
    high = value.astype(BF16).astype(F32)
    mid = (value - high).astype(BF16).astype(F32)
    low = value - high - mid
    return jnp.where(
        row == 0, high, jnp.where(row == 1, mid, jnp.where(row == 2, low, 0.0))
    ).astype(BF16)


def decode(tile):
    return jnp.sum(tile.astype(F32), axis=0, keepdims=True)


def adam_body(index, grad, second, new_second, pay, sums):
    step = pl.program_id(0)

    @pl.when(step == 0)
    def _():
        sums[...] = jnp.zeros_like(sums)

    g = grad[...].astype(F32)
    ns = 0.999 * second[...] + 0.001 * g * g
    new_second[...] = ns
    d = g / (jnp.sqrt(ns) + 1e-08)
    q = d * d
    for c in range(LB * TB):
        cols = slice(c * LANES, (c + 1) * LANES)
        pay[2 * step, c] = g[:SUB, cols].astype(BF16)
        pay[2 * step + 1, c] = g[SUB:, cols].astype(BF16)
        sums[c // TB] += q[:SUB, cols] + q[SUB:, cols]

    @pl.when(step == ROW_DEV // 16 - 1)
    def _():
        lane = lax.broadcasted_iota(jnp.int32, (1, LANES), 1)
        first = index[0] * LB
        value = jnp.zeros((1, LANES), F32)
        for j in range(LB):
            value = jnp.where(lane == first + j, jnp.sum(sums[j]), value)
        tile = encode(value)
        for g in range(MD):
            pay[g, LB * TB] = tile


def adam(index, gradient, second_moment):
    rows = pl.BlockSpec((16, LOCAL), lambda i: (i, 0))
    pay = (MD, LB * TB + 1, SUB, LANES)
    return pl.pallas_call(
        adam_body,
        grid=(ROW_DEV // 16,),
        out_shape=(struct(ROW_DEV, LOCAL, dtype=F32), struct(*pay)),
        in_specs=[pl.BlockSpec(memory_space=pltpu.SMEM), rows, rows],
        out_specs=(rows, pl.BlockSpec(pay, lambda i: (0, 0, 0, 0))),
        scratch_shapes=[pltpu.VMEM((LB, SUB, LANES), F32)],
        compiler_params=pltpu.CompilerParams(vmem_limit_bytes=16 * 1024 * 1024),
        name="adam",
    )(index, gradient, second_moment)


def spread_body(plan, got, out):
    tile = got[0, LB * TB].astype(F32)
    for m in range(1, MD):
        tile += got[m, LB * TB].astype(F32)
    tile = tile.astype(BF16)
    for z in range(ZD):
        for y in range(YDIM):
            j = plan[INV + z * YDIM + y]
            out[z, y * TB : (y + 1) * TB] = got[j // LB, pl.ds(lax.rem(j, LB) * TB, TB)]
        out[z, YDIM * TB] = tile


def pack_body(plan, left, right, moment, after, *outs):
    for s in range(MD):
        t = plan[OUT + s]
        outs[s][0] = left[t]
        outs[s][1] = right[t]
        outs[s][2] = moment[t]


def plane_body(got, *refs):
    out = refs[-1]
    for b in range(BANDS):
        total = decode(got[b * ZZ, YDIM * TB])
        for k in range(1, ZZ):
            total += decode(got[b * ZZ + k, YDIM * TB])
        tile = encode(total)
        for y in range(YDIM):
            for k in range(ZZ):
                out[y * BANDS + b, k * TB : (k + 1) * TB] = got[
                    b * ZZ + k, y * TB : (y + 1) * TB
                ]
            out[y * BANDS + b, ZZ * TB] = tile


def block_body(plan, got, *refs):
    packed, (back, block, moment), (left, right, applied, prod) = (
        refs[:MD],
        refs[MD : MD + 3],
        refs[MD + 3 :],
    )
    me = plan[OTHER]
    for k in range(ZZ):
        for y in range(YDIM):
            for g in range(0, MD, 2):
                row = (k * YDIM + y) * ROW_DEV + g * SUB
                for c in range(TB):
                    pair = [got[y * MD + g + i, k * TB + c].astype(F32) for i in range(2)]
                    block[row : row + 16, c * LANES : (c + 1) * LANES] = jnp.concatenate(
                        pair, axis=0
                    ).astype(BF16)
    for s in range(MD):
        rows = pl.ds(pl.multiple_of(lax.rem(me - s + MD, MD) * ROW_DEV, ROW_DEV), ROW_DEV)
        left[rows, :] = packed[s][0]
        right[rows, :] = packed[s][1]
    adam = decode(got[0, ZZ * TB])
    for y in range(1, YDIM):
        adam += decode(got[y * MD, ZZ * TB])
    lane = lax.broadcasted_iota(jnp.int32, (1, LANES), 1)
    adam = jnp.sum(jnp.where(lane == plan[OTHER + 1], adam, 0.0), keepdims=True)
    applied[...] = jnp.dot(left[...], block[...], preferred_element_type=F32).astype(BF16)
    p = jnp.dot(applied[...], right[...], preferred_element_type=F32)
    prod[...] = p
    norm = jnp.sum(p * p, keepdims=True)
    graft = jnp.sqrt(adam / AREA) / jnp.sqrt(norm / AREA + 1e-06)
    total = jnp.zeros((ROW_DEV, BLK), F32)
    for s in range(MD):
        rows = pl.ds(pl.multiple_of(lax.rem(me - s + MD, MD) * ROW_DEV, ROW_DEV), ROW_DEV)
        f = 0.9 * packed[s][2].astype(F32) + graft * prod[rows, :]
        total += f * f
        moment[rows, :] = f.astype(BF16)
    square = jnp.sum(total, keepdims=True)
    square = jnp.where(plan[OTHER + 2] > 0, square, 0.0)
    tile = encode(jnp.broadcast_to(square, (1, LANES)))
    for y in range(YDIM):
        for g in range(0, MD, 2):
            for k in range(ZZ):
                row = (k * YDIM + y) * ROW_DEV + g * SUB
                for c in range(TB):
                    both = moment[row : row + 16, c * LANES : (c + 1) * LANES].astype(F32)
                    back[y * MD + g, k * TB + c] = both[:SUB].astype(BF16)
                    back[y * MD + g + 1, k * TB + c] = both[SUB:].astype(BF16)
            back[y * MD + g, ZZ * TB] = tile
            back[y * MD + g + 1, ZZ * TB] = tile


def stats_body(plan, block, moment, after, *refs):
    outs, (left, right) = refs[:MD], refs[MD:]
    me = plan[OTHER]
    left[...] = lax.dot_general(
        block[...], block[...], (((1,), (1,)), ((), ())), preferred_element_type=F32
    ).astype(BF16)
    right[...] = lax.dot_general(
        block[...], block[...], (((0,), (0,)), ((), ())), preferred_element_type=F32
    ).astype(BF16)
    for s in range(MD):
        rows = pl.ds(pl.multiple_of(lax.rem(me + s, MD) * ROW_DEV, ROW_DEV), ROW_DEV)
        outs[s][0] = left[rows, :]
        outs[s][1] = right[rows, :]
        outs[s][2] = moment[rows, :]


def unplane_body(got, out):
    total = decode(got[0, ZZ * TB])
    for i in range(1, YDIM * BANDS):
        total += decode(got[i, ZZ * TB])
    tile = encode(total)
    for b in range(BANDS):
        for k in range(ZZ):
            for y in range(YDIM):
                out[b * ZZ + k, y * TB : (y + 1) * TB] = got[
                    y * BANDS + b, k * TB : (k + 1) * TB
                ]
            out[b * ZZ + k, YDIM * TB] = tile


def place_body(plan, got, *refs):
    out = refs[-1]
    total = decode(got[0, YDIM * TB])
    for z in range(1, ZD):
        total += decode(got[z, YDIM * TB])
    clip = jnp.minimum(1.0, 0.5 * math.sqrt(ROWS * COLS) / jnp.sqrt(total))
    for m in range(MD):
        for i in range(LB):
            o = plan[BAND + m * LB + i]
            z, y = o // YDIM, lax.rem(o, YDIM)
            piece = got[z, pl.ds(y * TB, TB)].astype(F32)
            for c in range(TB):
                col = (i * TB + c) * LANES
                out[m, :, col : col + LANES] = (clip * piece[c]).astype(BF16)


def finish_body(plan, left, right, *refs):
    parts, (new_left, new_right, new_moment) = refs[:MD], refs[MD:]
    for s in range(MD):
        t = plan[IN + s]

        @pl.when(t >= 0)
        def _():
            new_left[t] = 0.95 * left[t] + 0.05 * parts[s][0].astype(F32)
            new_right[t] = 0.95 * right[t] + 0.05 * parts[s][1].astype(F32)
            new_moment[t] = parts[s][2]


def make_plan(owner_table):
    z = lax.axis_index("z")
    m = lax.axis_index("m")
    owner = z * YDIM + lax.axis_index("y")
    table = owner_table.reshape(BANDS, CB)
    band_owner = lax.dynamic_index_in_dim(table, z // ZZ, 0, keepdims=False)
    iota = lambda n: jnp.arange(n, dtype=jnp.int32)
    held = band_owner[None, :] == iota(OWNERS)[:, None]
    inverse = jnp.sum(jnp.where(held, iota(CB)[None, :], 0), axis=1)
    mine = table == owner
    has = jnp.sum(mine.astype(jnp.int32), axis=1)
    column = jnp.sum(jnp.where(mine, iota(CB)[None, :], 0), axis=1)
    slot = jnp.sum(jnp.where(iota(BANDS)[None, :] < iota(BANDS)[:, None], has[None, :], 0), axis=1)
    slot = jnp.minimum(slot, SLOTS - 1)
    pick = lambda at, values: jnp.sum(
        jnp.where(iota(BANDS)[None, :] == at[:, None], values[None, :], 0), axis=1
    )
    to = pick(lax.rem(m + iota(MD), MD), slot)
    source = pick(lax.rem(m - iota(MD) + MD, MD), jnp.where(has > 0, slot, -1))
    self = m[None]
    other = jnp.concatenate([self, pick(self, column), pick(self, has)])
    plan = jnp.concatenate([inverse, band_owner, to, source, other])
    return jnp.pad(plan, (0, PLAN - plan.shape[0])).astype(jnp.int32)


def shift(parts):
    moved = [parts[0]]
    for s in range(1, MD):
        moved.append(lax.ppermute(parts[s], "m", [(i, (i + s) % MD) for i in range(MD)]))
    return moved


def shards(
    gradient, second_moment, owner_table, left_stats, right_stats, left_root, right_root, momentum
):
    plan = make_plan(owner_table)
    slab = [struct(3, ROW_DEV, BLK)] * MD
    square = (BLK, BLK)

    index = lax.axis_index("m")[None]
    new_second, pay = adam(index, gradient, second_moment)
    got = lax.all_to_all(pay, "m", 0, 0, tiled=True)
    (pay,) = call(
        spread_body, "sv", [struct(ZD, YDIM * TB + 1, SUB, LANES)], [plan, got], name="spread"
    )
    packed = call(
        pack_body,
        "svvva",
        slab,
        [plan, left_root[0], right_root[0], momentum[0], pay],
        name="pack",
    )
    got = lax.all_to_all(pay, "z", 0, 0, tiled=True)
    packed = shift(packed)
    (pay,) = call(
        plane_body,
        "v" + "a" * (MD - 1),
        [struct(YDIM * BANDS, ZZ * TB + 1, SUB, LANES)],
        [got, *packed[1:]],
        name="plane",
    )
    got = lax.all_to_all(pay, ("y", "m"), 0, 0, tiled=True)
    back, block, moment = call(
        block_body,
        "sv" + "v" * MD,
        [struct(YDIM * MD, ZZ * TB + 1, SUB, LANES), struct(*square), struct(*square)],
        [plan, got, *packed],
        scratch=[pltpu.VMEM(square, BF16)] * 3 + [pltpu.VMEM(square, F32)],
        flops=4 * BLK**3,
        vmem=24,
        name="block",
    )
    got = lax.all_to_all(back, ("y", "m"), 0, 0, tiled=True)
    (pay,) = call(
        unplane_body, "v", [struct(ZD, YDIM * TB + 1, SUB, LANES)], [got], name="unplane"
    )
    results = call(
        stats_body,
        "svva",
        slab,
        [plan, block, moment, pay],
        scratch=[pltpu.VMEM(square, BF16)] * 2,
        flops=4 * BLK**3,
        name="stats",
    )
    got = lax.all_to_all(pay, "z", 0, 0, tiled=True)
    results = shift(results)
    (pay,) = call(
        place_body,
        "sv" + "a" * (MD - 1),
        [struct(MD, SUB, LOCAL)],
        [plan, got, *results[1:]],
        name="place",
    )
    update = lax.all_to_all(pay, "m", 0, 0, tiled=True).reshape(ROW_DEV, LOCAL)
    stat = struct(SLOTS, ROW_DEV, BLK, dtype=F32)
    new_left, new_right, new_moment = call(
        finish_body,
        "svv" + "v" * MD,
        [stat, stat, struct(SLOTS, ROW_DEV, BLK)],
        [plan, left_stats[0], right_stats[0], *results],
        name="finish",
    )
    return update, new_second, new_left[None], new_right[None], new_moment[None]


def solution(mesh):
    owners, groups = mesh.devices.shape
    inner = Mesh(mesh.devices.reshape(owners // YDIM, YDIM, groups), AXES)
    wide = P(("z", "y"), "m")
    stats = P(("z", "y"), None, "m", None)
    return jax.shard_map(
        shards,
        mesh=inner,
        in_specs=(wide, wide, P(), stats, stats, stats, stats, stats),
        out_specs=(wide, wide, stats, stats, stats),
        check_vma=False,
    )
```

```python
import math

import jax
import jax.numpy as jnp
from jax import lax
from jax.experimental import pallas as pl
from jax.experimental.pallas import tpu as pltpu
from jax.sharding import Mesh
from jax.sharding import PartitionSpec as P

BLK = 512
ROWS = 4096
COLS = 16384
YDIM = 4
AXES = ("z", "y", "m")

ZD, MD = 16, 8
OWNERS = ZD * YDIM
BANDS = ROWS // BLK
CB = COLS // BLK
ZZ = ZD // BANDS
SUB = 8
ROW_DEV = 64
LOCAL = COLS // MD
LB = LOCAL // BLK
LANES = 128
TB = BLK // LANES
SLOTS = 4
AREA = BLK * BLK
SHIFTS = (4, 5, 3, 6, 2, 7, 1)
CHUNKS = 4

BF16, F32 = jnp.bfloat16, jnp.float32


def struct(*shape, dtype=BF16):
    return jax.ShapeDtypeStruct(shape, dtype)


def hold_shapes(hold):
    return [struct(*a.shape, dtype=a.dtype) for a in hold]


def call(body, specs, outs, args, scratch=(), vmem=16, flops=0, name=None, stream=False, hold=()):
    space = {"v": pltpu.VMEM, "s": pltpu.SMEM, "a": pl.ANY}
    size = sum(o.size * o.dtype.itemsize for o in outs)
    size += sum(a.size * a.dtype.itemsize for a, k in zip(args, specs) if k == "v")
    first = len(args)
    specs, args, outs = specs + "a" * len(hold), [*args, *hold], [*outs, *hold_shapes(hold)]
    scratch = list(scratch)
    if stream:
        scratch += [pltpu.VMEM(outs[0].shape, outs[0].dtype), pltpu.SemaphoreType.DMA((CHUNKS + 1,))]
    return pl.pallas_call(
        body,
        out_shape=tuple(outs),
        in_specs=[pl.BlockSpec(memory_space=space[k]) for k in specs],
        out_specs=tuple(pl.BlockSpec(memory_space=space["a" if stream else "v"]) for _ in outs),
        input_output_aliases={first + i: 1 + i for i in range(len(hold))},
        scratch_shapes=scratch,
        compiler_params=pltpu.CompilerParams(vmem_limit_bytes=vmem * 1024 * 1024),
        cost_estimate=pl.CostEstimate(flops=flops, bytes_accessed=size, transcendentals=0),
        name=name,
    )(*args)


def stream(fill, out, buffer, sems):
    size = buffer.shape[0] // CHUNKS
    copies = []
    for i in range(CHUNKS):
        for row in range(i * size, (i + 1) * size):
            fill(row)
        rows = pl.ds(i * size, size)
        copy = pltpu.make_async_copy(buffer.at[rows], out.at[rows], sems.at[i])
        copy.start()
        copies.append(copy)
    for copy in copies:
        copy.wait()


def join(first, second):
    return jnp.concatenate([first, second], axis=0)


def encode(value):
    value = jnp.broadcast_to(value, (SUB, LANES))
    row = lax.broadcasted_iota(jnp.int32, (SUB, LANES), 0)
    high = value.astype(BF16).astype(F32)
    mid = (value - high).astype(BF16).astype(F32)
    low = value - high - mid
    return jnp.where(
        row == 0, high, jnp.where(row == 1, mid, jnp.where(row == 2, low, 0.0))
    ).astype(BF16)


def decode(tile):
    return jnp.sum(tile.astype(F32), axis=0, keepdims=True)


def adam_body(index, grad, second, new_second, tile, sums):
    step = pl.program_id(0)

    @pl.when(step == 0)
    def _():
        sums[...] = jnp.zeros_like(sums)

    g = grad[...].astype(F32)
    ns = 0.999 * second[...] + 0.001 * g * g
    new_second[...] = ns
    d = g / (jnp.sqrt(ns) + 1e-08)
    q = d * d
    for c in range(LB * TB):
        cols = slice(c * LANES, (c + 1) * LANES)
        sums[c // TB] += q[:SUB, cols] + q[SUB:, cols]

    @pl.when(step == ROW_DEV // 16 - 1)
    def _():
        lane = lax.broadcasted_iota(jnp.int32, (1, LANES), 1)
        first = index[0] * LB
        value = jnp.zeros((1, LANES), F32)
        for j in range(LB):
            value = jnp.where(lane == first + j, jnp.sum(sums[j]), value)
        tile[...] = encode(value)


def adam(index, gradient, second_moment):
    rows = pl.BlockSpec((16, LOCAL), lambda i: (i, 0))
    return pl.pallas_call(
        adam_body,
        grid=(ROW_DEV // 16,),
        out_shape=(struct(ROW_DEV, LOCAL, dtype=F32), struct(SUB, LANES)),
        in_specs=[pl.BlockSpec(memory_space=pltpu.SMEM), rows, rows],
        out_specs=(rows, pl.BlockSpec((SUB, LANES), lambda i: (0, 0))),
        scratch_shapes=[pltpu.VMEM((LB, SUB, LANES), F32)],
        compiler_params=pltpu.CompilerParams(vmem_limit_bytes=16 * 1024 * 1024),
        name="adam",
    )(index, gradient, second_moment)


def spread_body(inverse, tile, got, out, buffer, sems):
    def fill(z):
        for y in range(YDIM):
            j = inverse[z * YDIM + y]
            lanes = pl.ds(pl.multiple_of((j & (LB - 1)) * BLK, BLK), BLK)
            piece = got[j >> 2, :, lanes]
            for c in range(TB):
                buffer[z, y * TB + c] = piece[:, c * LANES : (c + 1) * LANES]
        buffer[z, YDIM * TB] = tile[...]

    stream(fill, out, buffer, sems)


def pack_body(to, left, right, moment, after, *outs):
    for s in range(MD):
        t = to[s]
        outs[s][0] = left[t]
        outs[s][1] = right[t]
        outs[s][2] = moment[t]


def plane_body(got, *refs):
    out, buffer, sems = refs[-3:]
    tiles = []
    for b in range(BANDS):
        total = decode(got[b * ZZ, YDIM * TB])
        for k in range(1, ZZ):
            total += decode(got[b * ZZ + k, YDIM * TB])
        tiles.append(encode(total))

    def fill(row):
        y, b = divmod(row, BANDS)
        for k in range(ZZ):
            buffer[row, k * TB : (k + 1) * TB] = got[b * ZZ + k, y * TB : (y + 1) * TB]
        buffer[row, ZZ * TB] = tiles[b]

    stream(fill, out, buffer, sems)


def roots_body(other, *refs):
    parts, outs = refs[:MD], refs[MD:]
    for s in range(MD):
        source = lax.rem(other[0] - s + MD, MD)
        rows = pl.ds(pl.multiple_of(source * ROW_DEV, ROW_DEV), ROW_DEV)
        for i in range(3):
            outs[i][rows, :] = parts[s][i]


def assemble(got, block):
    for k in range(ZZ):
        for y in range(YDIM):
            for g in range(0, MD, 2):
                row = (k * YDIM + y) * ROW_DEV + g * SUB
                for c in range(TB):
                    block[row : row + 16, c * LANES : (c + 1) * LANES] = join(
                        got[y * MD + g, k * TB + c], got[y * MD + g + 1, k * TB + c]
                    )


def block_body(masks, got, left, right, old, out, block, applied, prod, buffer, sems):
    assemble(got, block)
    adam = got[0, ZZ * TB].astype(F32)
    for i in range(1, YDIM * MD):
        adam += got[i, ZZ * TB].astype(F32)
    adam = jnp.sum(jnp.where(masks[:1, :] > 0, decode(adam), 0.0), keepdims=True)
    applied[...] = jnp.dot(left[...], block[...], preferred_element_type=F32).astype(BF16)
    p = jnp.dot(applied[...], right[...], preferred_element_type=F32)
    prod[...] = p
    norm = jnp.sum(p * p, keepdims=True)
    graft = jnp.sqrt(adam / AREA) / jnp.sqrt(norm / AREA + 1e-06)
    total = jnp.zeros((16, BLK), F32)
    copies = []
    for y in range(YDIM):
        for g in range(0, MD, 2):
            for k in range(ZZ):
                row = (k * YDIM + y) * ROW_DEV + g * SUB
                rows = slice(row, row + 16)
                f = 0.9 * old[rows, :].astype(F32) + graft * prod[rows, :]
                total += f * f
                for c in range(TB):
                    cols = slice(c * LANES, (c + 1) * LANES)
                    buffer[y * MD + g, k * TB + c] = f[:SUB, cols].astype(BF16)
                    buffer[y * MD + g + 1, k * TB + c] = f[SUB:, cols].astype(BF16)
        if y < YDIM - 1:
            part = (pl.ds(y * MD, MD), pl.ds(0, ZZ * TB))
            copies.append(pltpu.make_async_copy(buffer.at[part], out.at[part], sems.at[y]))
            copies[-1].start()
    square = jnp.broadcast_to(jnp.sum(total, keepdims=True), (1, LANES))
    tile = encode(jnp.where(masks[1:2, :] > 0, square, 0.0))
    for slot in range(YDIM * MD):
        buffer[slot, ZZ * TB] = tile
    last = (YDIM - 1) * MD
    rest = pl.ds(last, MD)
    copies.append(pltpu.make_async_copy(buffer.at[rest], out.at[rest], sems.at[YDIM - 1]))
    part = (pl.ds(0, last), pl.ds(ZZ * TB, 1))
    copies.append(pltpu.make_async_copy(buffer.at[part], out.at[part], sems.at[YDIM]))
    for copy in copies[-2:]:
        copy.start()
    for copy in copies:
        copy.wait()


def stats_body(other, got, moment, *refs):
    outs, (block, left, right) = refs[:MD], refs[MD:]
    assemble(got, block)
    left[...] = lax.dot_general(
        block[...], block[...], (((1,), (1,)), ((), ())), preferred_element_type=F32
    ).astype(BF16)
    right[...] = lax.dot_general(
        block[...], block[...], (((0,), (0,)), ((), ())), preferred_element_type=F32
    ).astype(BF16)
    for s, out in enumerate(outs):
        to = lax.rem(other[0] + s, MD)
        rows = pl.ds(pl.multiple_of(to * ROW_DEV, ROW_DEV), ROW_DEV)
        out[0] = left[rows, :]
        out[1] = right[rows, :]
        first, tiles = lax.rem(to, YDIM) * MD, (to // YDIM) * TB
        for g in range(0, MD, 2):
            for c in range(TB):
                out[2, g * SUB : g * SUB + 16, c * LANES : (c + 1) * LANES] = join(
                    moment[first + g, tiles + c], moment[first + g + 1, tiles + c]
                )


def unplane_body(got, *refs):
    out, (buffer, sems) = refs[MD - 1], refs[-2:]
    total = got[0, ZZ * TB].astype(F32)
    for i in range(1, YDIM * BANDS):
        total += got[i, ZZ * TB].astype(F32)
    tile = encode(decode(total))

    def fill(z):
        b, k = divmod(z, ZZ)
        for y in range(YDIM):
            buffer[z, y * TB : (y + 1) * TB] = got[y * BANDS + b, k * TB : (k + 1) * TB]
        buffer[z, YDIM * TB] = tile

    stream(fill, out, buffer, sems)


def place_body(band_owner, got, *refs):
    out, buffer, sems = refs[-3:]

    def fill(m):
        for i in range(LB):
            o = band_owner[m * LB + i]
            z, first = o >> 2, (o & (YDIM - 1)) * TB
            for c in range(TB):
                col = (i * TB + c) * LANES
                buffer[m, :, col : col + LANES] = got[z, first + c]

    stream(fill, out, buffer, sems)


def norm_body(got, out):
    total = got[0, YDIM * TB].astype(F32)
    for z in range(1, ZD):
        total += got[z, YDIM * TB].astype(F32)
    out[...] = jnp.minimum(1.0, 0.5 * math.sqrt(ROWS * COLS) / jnp.sqrt(decode(total)))


def finish_body(source, left, right, *refs):
    parts, (new_left, new_right, new_moment) = refs[:MD], refs[MD:]
    for s in range(MD):
        t = source[s]

        @pl.when(t >= 0)
        def _():
            new_left[t] = 0.95 * left[t] + 0.05 * parts[s][0].astype(F32)
            new_right[t] = 0.95 * right[t] + 0.05 * parts[s][1].astype(F32)
            new_moment[t] = parts[s][2]


def make_plan(owner_table):
    z = lax.axis_index("z")
    m = lax.axis_index("m")
    owner = z * YDIM + lax.axis_index("y")
    table = owner_table.reshape(BANDS, CB)
    band_owner = lax.dynamic_index_in_dim(table, z // ZZ, 0, keepdims=False)
    iota = lambda n: jnp.arange(n, dtype=jnp.int32)
    held = band_owner[None, :] == iota(OWNERS)[:, None]
    inverse = jnp.sum(jnp.where(held, iota(CB)[None, :], 0), axis=1)
    mine = table == owner
    has = jnp.sum(mine.astype(jnp.int32), axis=1)
    column = jnp.sum(jnp.where(mine, iota(CB)[None, :], 0), axis=1)
    slot = jnp.sum(jnp.where(iota(BANDS)[None, :] < iota(BANDS)[:, None], has[None, :], 0), axis=1)
    slot = jnp.minimum(slot, SLOTS - 1)
    pick = lambda at, values: jnp.sum(
        jnp.where(iota(BANDS)[None, :] == at[:, None], values[None, :], 0), axis=1
    )
    to = pick(lax.rem(m + iota(MD), MD), slot)
    source = pick(lax.rem(m - iota(MD) + MD, MD), jnp.where(has > 0, slot, -1))
    self = m[None]
    lane = jnp.where(iota(LANES) == pick(self, column), 1.0, 0.0)
    held = jnp.broadcast_to(pick(self, has), (LANES,)).astype(F32)
    masks = jnp.pad(jnp.stack([lane, held]), ((0, SUB - 2), (0, 0)))
    return inverse, band_owner, to, source, self, masks


def shift(part, s):
    return lax.ppermute(part, "m", [(i, (i + s) % MD) for i in range(MD)])


def shards(
    gradient, second_moment, owner_table, left_stats, right_stats, left_root, right_root, momentum
):
    inverse, band_owner, to, source, other, masks = make_plan(owner_table)
    square = (BLK, BLK)

    got = lax.all_to_all(gradient.reshape(MD, SUB, LOCAL), "m", 0, 0, tiled=True)
    new_second, tile = adam(lax.axis_index("m")[None], gradient, second_moment)
    (pay,) = call(
        spread_body,
        "svv",
        [struct(ZD, YDIM * TB + 1, SUB, LANES)],
        [inverse, tile, got],
        name="spread",
        stream=True,
    )
    packed = call(
        pack_body,
        "svvva",
        [struct(3, ROW_DEV, BLK)] * MD,
        [to, left_root[0], right_root[0], momentum[0], pay],
        name="pack",
    )
    got = lax.all_to_all(pay, "z", 0, 0, tiled=True)
    moved = {0: packed[0]}
    for s in SHIFTS:
        moved[s] = shift(packed[s], s)
    (pay,) = call(
        plane_body,
        "v" + "a" * len(SHIFTS),
        [struct(YDIM * BANDS, ZZ * TB + 1, SUB, LANES)],
        [got, *(moved[s] for s in SHIFTS)],
        name="plane",
        stream=True,
    )
    got = lax.all_to_all(pay, ("y", "m"), 0, 0, tiled=True)
    left, right, old = call(
        roots_body,
        "s" + "v" * MD,
        [struct(*square)] * 3,
        [other, *(moved[s] for s in range(MD))],
        name="roots",
    )
    whole = got
    (back,) = call(
        block_body,
        "vvvvv",
        [struct(YDIM * MD, ZZ * TB + 1, SUB, LANES)],
        [masks, whole, left, right, old],
        scratch=[
            pltpu.VMEM(square, BF16),
            pltpu.VMEM(square, BF16),
            pltpu.VMEM(square, F32),
        ],
        flops=4 * BLK**3,
        vmem=24,
        name="block",
        stream=True,
    )
    got = lax.all_to_all(back, ("y", "m"), 0, 0, tiled=True)
    parts = call(
        stats_body,
        "svv",
        [struct(3, ROW_DEV, BLK)] * MD,
        [other, whole, back],
        scratch=[pltpu.VMEM(square, BF16)] * 3,
        flops=4 * BLK**3,
        name="stats",
    )
    pay, *held = call(
        unplane_body,
        "v",
        [struct(ZD, YDIM * TB + 1, SUB, LANES)],
        [got],
        name="unplane",
        stream=True,
        hold=parts[1:],
    )
    got = lax.all_to_all(pay, "z", 0, 0, tiled=True)
    results = {0: parts[0]}
    for s in SHIFTS:
        results[s] = shift(held[s - 1], s)
    (pay,) = call(
        place_body,
        "sv" + "a" * len(SHIFTS),
        [struct(MD, SUB, LOCAL)],
        [band_owner, got, *(results[s] for s in SHIFTS)],
        name="place",
        stream=True,
    )
    (clip,) = call(norm_body, "v", [struct(1, LANES, dtype=F32)], [got], name="norm")
    placed = lax.all_to_all(pay, "m", 0, 0, tiled=True).reshape(ROW_DEV, LOCAL)
    update = (clip[0, 0] * placed.astype(F32)).astype(BF16)
    stat = struct(SLOTS, ROW_DEV, BLK, dtype=F32)
    new_left, new_right, new_moment = call(
        finish_body,
        "svv" + "v" * MD,
        [stat, stat, struct(SLOTS, ROW_DEV, BLK)],
        [source, left_stats[0], right_stats[0], *(results[s] for s in range(MD))],
        name="finish",
    )
    return update, new_second, new_left[None], new_right[None], new_moment[None]


def solution(mesh):
    owners, groups = mesh.devices.shape
    inner = Mesh(mesh.devices.reshape(owners // YDIM, YDIM, groups), AXES)
    wide = P(("z", "y"), "m")
    stats = P(("z", "y"), None, "m", None)
    return jax.shard_map(
        shards,
        mesh=inner,
        in_specs=(wide, wide, P(), stats, stats, stats, stats, stats),
        out_specs=(wide, wide, stats, stats, stats),
        check_vma=False,
    )
```

```python
import math

import jax
import jax.numpy as jnp
from jax import lax
from jax.experimental import pallas as pl
from jax.experimental.pallas import tpu as pltpu
from jax.sharding import Mesh
from jax.sharding import PartitionSpec as P

BLK = 512
ROWS = 4096
COLS = 16384
YDIM = 4
AXES = ("z", "y", "m")

ZD, MD = 16, 8
OWNERS = ZD * YDIM
BANDS = ROWS // BLK
CB = COLS // BLK
ZZ = ZD // BANDS
SUB = 8
ROW_DEV = 64
LOCAL = COLS // MD
LB = LOCAL // BLK
LANES = 128
TB = BLK // LANES
SLOTS = 4
AREA = BLK * BLK
SHIFTS = (4, 5, 3, 6, 2, 7, 1)
CHUNKS = 4

BF16, F32 = jnp.bfloat16, jnp.float32


def struct(*shape, dtype=BF16):
    return jax.ShapeDtypeStruct(shape, dtype)


def hold_shapes(hold):
    return [struct(*a.shape, dtype=a.dtype) for a in hold]


def call(
    body,
    specs,
    outs,
    args,
    scratch=(),
    vmem=16,
    flops=0,
    name=None,
    stream=False,
    hold=(),
    prefetch=False,
):
    space = {"v": pltpu.VMEM, "s": pltpu.SMEM, "a": pl.ANY}
    size = sum(o.size * o.dtype.itemsize for o in outs)
    size += sum(a.size * a.dtype.itemsize for a, k in zip(args, specs) if k == "v")
    first = len(args)
    specs, args, outs = specs + "a" * len(hold), [*args, *hold], [*outs, *hold_shapes(hold)]
    scratch = list(scratch)
    if stream:
        scratch += [pltpu.VMEM(outs[0].shape, outs[0].dtype), pltpu.SemaphoreType.DMA((CHUNKS + 1,))]
    count = specs.count("s") if prefetch else 0
    return pl.pallas_call(
        body,
        out_shape=tuple(outs),
        grid_spec=pltpu.PrefetchScalarGridSpec(
            num_scalar_prefetch=count,
            grid=(),
            in_specs=[pl.BlockSpec(memory_space=space[k]) for k in specs[count:]],
            out_specs=tuple(
                pl.BlockSpec(memory_space=space["a" if stream else "v"]) for _ in outs
            ),
            scratch_shapes=scratch,
        ),
        input_output_aliases={first + i: 1 + i for i in range(len(hold))},
        compiler_params=pltpu.CompilerParams(vmem_limit_bytes=vmem * 1024 * 1024),
        cost_estimate=pl.CostEstimate(flops=flops, bytes_accessed=size, transcendentals=0),
        name=name,
    )(*args)


def stream(fill, out, buffer, sems):
    size = buffer.shape[0] // CHUNKS
    copies = []
    for i in range(CHUNKS):
        for row in range(i * size, (i + 1) * size):
            fill(row)
        rows = pl.ds(i * size, size)
        copy = pltpu.make_async_copy(buffer.at[rows], out.at[rows], sems.at[i])
        copy.start()
        copies.append(copy)
    for copy in copies:
        copy.wait()


def join(first, second):
    return jnp.concatenate([first, second], axis=0)


def encode(value):
    value = jnp.broadcast_to(value, (SUB, LANES))
    row = lax.broadcasted_iota(jnp.int32, (SUB, LANES), 0)
    high = value.astype(BF16).astype(F32)
    mid = (value - high).astype(BF16).astype(F32)
    low = value - high - mid
    return jnp.where(
        row == 0, high, jnp.where(row == 1, mid, jnp.where(row == 2, low, 0.0))
    ).astype(BF16)


def decode(tile):
    return jnp.sum(tile.astype(F32), axis=0, keepdims=True)


def adam_body(index, grad, second, new_second, tile, sums):
    step = pl.program_id(0)

    @pl.when(step == 0)
    def _():
        sums[...] = jnp.zeros_like(sums)

    g = grad[...].astype(F32)
    ns = 0.999 * second[...] + 0.001 * g * g
    new_second[...] = ns
    d = g / (jnp.sqrt(ns) + 1e-08)
    q = d * d
    for c in range(LB * TB):
        cols = slice(c * LANES, (c + 1) * LANES)
        sums[c // TB] += q[:SUB, cols] + q[SUB:, cols]

    @pl.when(step == ROW_DEV // 16 - 1)
    def _():
        lane = lax.broadcasted_iota(jnp.int32, (1, LANES), 1)
        first = index[0] * LB
        value = jnp.zeros((1, LANES), F32)
        for j in range(LB):
            value = jnp.where(lane == first + j, jnp.sum(sums[j]), value)
        tile[...] = encode(value)


def adam(index, gradient, second_moment):
    rows = pl.BlockSpec((16, LOCAL), lambda i: (i, 0))
    return pl.pallas_call(
        adam_body,
        grid=(ROW_DEV // 16,),
        out_shape=(struct(ROW_DEV, LOCAL, dtype=F32), struct(SUB, LANES)),
        in_specs=[pl.BlockSpec(memory_space=pltpu.SMEM), rows, rows],
        out_specs=(rows, pl.BlockSpec((SUB, LANES), lambda i: (0, 0))),
        scratch_shapes=[pltpu.VMEM((LB, SUB, LANES), F32)],
        compiler_params=pltpu.CompilerParams(vmem_limit_bytes=16 * 1024 * 1024),
        name="adam",
    )(index, gradient, second_moment)


def spread_body(inverse, tile, got, before, out, buffer, sems):
    def fill(z):
        for y in range(YDIM):
            j = inverse[z * YDIM + y]
            lanes = pl.ds(pl.multiple_of((j & (LB - 1)) * BLK, BLK), BLK)
            piece = got[j >> 2, :, lanes]
            for c in range(TB):
                buffer[z, y * TB + c] = piece[:, c * LANES : (c + 1) * LANES]
        buffer[z, YDIM * TB] = tile[...]

    stream(fill, out, buffer, sems)


def pack_body(to, left, right, moment, after, *outs):
    for s in range(MD):
        t = to[s]
        outs[s][0] = left[t]
        outs[s][1] = right[t]
        outs[s][2] = moment[t]


def plane_body(got, *refs):
    out, buffer, sems = refs[-3:]
    tiles = []
    for b in range(BANDS):
        total = decode(got[b * ZZ, YDIM * TB])
        for k in range(1, ZZ):
            total += decode(got[b * ZZ + k, YDIM * TB])
        tiles.append(encode(total))

    def fill(row):
        y, b = divmod(row, BANDS)
        for k in range(ZZ):
            buffer[row, k * TB : (k + 1) * TB] = got[b * ZZ + k, y * TB : (y + 1) * TB]
        buffer[row, ZZ * TB] = tiles[b]

    stream(fill, out, buffer, sems)


def roots_body(other, *refs):
    parts, outs = refs[:MD], refs[MD:]
    for s in range(MD):
        source = lax.rem(other[0] - s + MD, MD)
        rows = pl.ds(pl.multiple_of(source * ROW_DEV, ROW_DEV), ROW_DEV)
        for i in range(3):
            outs[i][rows, :] = parts[s][i]


def assemble(got, block):
    for k in range(ZZ):
        for y in range(YDIM):
            for g in range(0, MD, 2):
                row = (k * YDIM + y) * ROW_DEV + g * SUB
                for c in range(TB):
                    block[row : row + 16, c * LANES : (c + 1) * LANES] = join(
                        got[y * MD + g, k * TB + c], got[y * MD + g + 1, k * TB + c]
                    )


def block_body(masks, got, left, right, old, out, block, applied, prod, buffer, sems):
    assemble(got, block)
    adam = got[0, ZZ * TB].astype(F32)
    for i in range(1, YDIM * MD):
        adam += got[i, ZZ * TB].astype(F32)
    adam = jnp.sum(jnp.where(masks[:1, :] > 0, decode(adam), 0.0), keepdims=True)
    applied[...] = jnp.dot(left[...], block[...], preferred_element_type=F32).astype(BF16)
    p = jnp.dot(applied[...], right[...], preferred_element_type=F32)
    prod[...] = p
    norm = jnp.sum(p * p, keepdims=True)
    graft = jnp.sqrt(adam / AREA) / jnp.sqrt(norm / AREA + 1e-06)
    total = jnp.zeros((16, BLK), F32)
    copies = []
    for y in range(YDIM):
        for g in range(0, MD, 2):
            for k in range(ZZ):
                row = (k * YDIM + y) * ROW_DEV + g * SUB
                rows = slice(row, row + 16)
                f = 0.9 * old[rows, :].astype(F32) + graft * prod[rows, :]
                total += f * f
                for c in range(TB):
                    cols = slice(c * LANES, (c + 1) * LANES)
                    buffer[y * MD + g, k * TB + c] = f[:SUB, cols].astype(BF16)
                    buffer[y * MD + g + 1, k * TB + c] = f[SUB:, cols].astype(BF16)
        if y < YDIM - 1:
            part = (pl.ds(y * MD, MD), pl.ds(0, ZZ * TB))
            copies.append(pltpu.make_async_copy(buffer.at[part], out.at[part], sems.at[y]))
            copies[-1].start()
    square = jnp.broadcast_to(jnp.sum(total, keepdims=True), (1, LANES))
    tile = encode(jnp.where(masks[1:2, :] > 0, square, 0.0))
    for slot in range(YDIM * MD):
        buffer[slot, ZZ * TB] = tile
    last = (YDIM - 1) * MD
    rest = pl.ds(last, MD)
    copies.append(pltpu.make_async_copy(buffer.at[rest], out.at[rest], sems.at[YDIM - 1]))
    part = (pl.ds(0, last), pl.ds(ZZ * TB, 1))
    copies.append(pltpu.make_async_copy(buffer.at[part], out.at[part], sems.at[YDIM]))
    for copy in copies[-2:]:
        copy.start()
    for copy in copies:
        copy.wait()


def stats_body(other, got, moment, *refs):
    outs, (block, left, right) = refs[:MD], refs[MD:]
    assemble(got, block)
    left[...] = lax.dot_general(
        block[...], block[...], (((1,), (1,)), ((), ())), preferred_element_type=F32
    ).astype(BF16)
    right[...] = lax.dot_general(
        block[...], block[...], (((0,), (0,)), ((), ())), preferred_element_type=F32
    ).astype(BF16)
    for s, out in enumerate(outs):
        to = lax.rem(other[0] + s, MD)
        rows = pl.ds(pl.multiple_of(to * ROW_DEV, ROW_DEV), ROW_DEV)
        out[0] = left[rows, :]
        out[1] = right[rows, :]
        first, tiles = lax.rem(to, YDIM) * MD, (to // YDIM) * TB
        for g in range(0, MD, 2):
            for c in range(TB):
                out[2, g * SUB : g * SUB + 16, c * LANES : (c + 1) * LANES] = join(
                    moment[first + g, tiles + c], moment[first + g + 1, tiles + c]
                )


def unplane_body(got, *refs):
    out, (buffer, sems) = refs[MD - 1], refs[-2:]
    total = got[0, ZZ * TB].astype(F32)
    for i in range(1, YDIM * BANDS):
        total += got[i, ZZ * TB].astype(F32)
    tile = encode(decode(total))

    def fill(z):
        b, k = divmod(z, ZZ)
        for y in range(YDIM):
            buffer[z, y * TB : (y + 1) * TB] = got[y * BANDS + b, k * TB : (k + 1) * TB]
        buffer[z, YDIM * TB] = tile

    stream(fill, out, buffer, sems)


def place_body(band_owner, got, *refs):
    out, buffer, sems = refs[-3:]

    def fill(m):
        for i in range(LB):
            o = band_owner[m * LB + i]
            z, first = o >> 2, (o & (YDIM - 1)) * TB
            for c in range(TB):
                col = (i * TB + c) * LANES
                buffer[m, :, col : col + LANES] = got[z, first + c]

    stream(fill, out, buffer, sems)


def norm_body(got, out):
    total = got[0, YDIM * TB].astype(F32)
    for z in range(1, ZD):
        total += got[z, YDIM * TB].astype(F32)
    out[...] = jnp.minimum(1.0, 0.5 * math.sqrt(ROWS * COLS) / jnp.sqrt(decode(total)))


def finish_body(source, left, right, *refs):
    parts, (new_left, new_right, new_moment) = refs[:MD], refs[MD:]
    for s in range(MD):
        t = source[s]

        @pl.when(t >= 0)
        def _():
            new_left[t] = 0.95 * left[t] + 0.05 * parts[s][0].astype(F32)
            new_right[t] = 0.95 * right[t] + 0.05 * parts[s][1].astype(F32)
            new_moment[t] = parts[s][2]


def make_plan(owner_table):
    z = lax.axis_index("z")
    m = lax.axis_index("m")
    owner = z * YDIM + lax.axis_index("y")
    table = owner_table.reshape(BANDS, CB)
    band_owner = lax.dynamic_index_in_dim(table, z // ZZ, 0, keepdims=False)
    iota = lambda n: jnp.arange(n, dtype=jnp.int32)
    held = band_owner[None, :] == iota(OWNERS)[:, None]
    inverse = jnp.sum(jnp.where(held, iota(CB)[None, :], 0), axis=1)
    mine = table == owner
    has = jnp.sum(mine.astype(jnp.int32), axis=1)
    column = jnp.sum(jnp.where(mine, iota(CB)[None, :], 0), axis=1)
    slot = jnp.sum(jnp.where(iota(BANDS)[None, :] < iota(BANDS)[:, None], has[None, :], 0), axis=1)
    slot = jnp.minimum(slot, SLOTS - 1)
    pick = lambda at, values: jnp.sum(
        jnp.where(iota(BANDS)[None, :] == at[:, None], values[None, :], 0), axis=1
    )
    to = pick(lax.rem(m + iota(MD), MD), slot)
    source = pick(lax.rem(m - iota(MD) + MD, MD), jnp.where(has > 0, slot, -1))
    self = m[None]
    lane = jnp.where(iota(LANES) == pick(self, column), 1.0, 0.0)
    held = jnp.broadcast_to(pick(self, has), (LANES,)).astype(F32)
    masks = jnp.pad(jnp.stack([lane, held]), ((0, SUB - 2), (0, 0)))
    return inverse, band_owner, to, source, self, masks


def shift(part, s):
    return lax.ppermute(part, "m", [(i, (i + s) % MD) for i in range(MD)])


def shards(
    gradient, second_moment, owner_table, left_stats, right_stats, left_root, right_root, momentum
):
    inverse, band_owner, to, source, other, masks = make_plan(owner_table)
    square = (BLK, BLK)

    got = lax.all_to_all(gradient.reshape(MD, SUB, LOCAL), "m", 0, 0, tiled=True)
    new_second, tile = adam(lax.axis_index("m")[None], gradient, second_moment)
    (pay,) = call(
        spread_body,
        "svva",
        [struct(ZD, YDIM * TB + 1, SUB, LANES)],
        [inverse, tile, got, to],
        name="spread",
        prefetch=True,
        stream=True,
    )
    packed = call(
        pack_body,
        "svvva",
        [struct(3, ROW_DEV, BLK)] * MD,
        [to, left_root[0], right_root[0], momentum[0], pay],
        name="pack",
        prefetch=True,
    )
    got = lax.all_to_all(pay, "z", 0, 0, tiled=True)
    moved = {0: packed[0]}
    for s in SHIFTS:
        moved[s] = shift(packed[s], s)
    (pay,) = call(
        plane_body,
        "v" + "a" * len(SHIFTS),
        [struct(YDIM * BANDS, ZZ * TB + 1, SUB, LANES)],
        [got, *(moved[s] for s in SHIFTS)],
        name="plane",
        stream=True,
    )
    got = lax.all_to_all(pay, ("y", "m"), 0, 0, tiled=True)
    left, right, old = call(
        roots_body,
        "s" + "v" * MD,
        [struct(*square)] * 3,
        [other, *(moved[s] for s in range(MD))],
        name="roots",
    )
    whole = got
    (back,) = call(
        block_body,
        "vvvvv",
        [struct(YDIM * MD, ZZ * TB + 1, SUB, LANES)],
        [masks, whole, left, right, old],
        scratch=[
            pltpu.VMEM(square, BF16),
            pltpu.VMEM(square, BF16),
            pltpu.VMEM(square, F32),
        ],
        flops=4 * BLK**3,
        vmem=24,
        name="block",
        stream=True,
    )
    got = lax.all_to_all(back, ("y", "m"), 0, 0, tiled=True)
    parts = call(
        stats_body,
        "svv",
        [struct(3, ROW_DEV, BLK)] * MD,
        [other, whole, back],
        scratch=[pltpu.VMEM(square, BF16)] * 3,
        flops=4 * BLK**3,
        name="stats",
    )
    pay, *held = call(
        unplane_body,
        "v",
        [struct(ZD, YDIM * TB + 1, SUB, LANES)],
        [got],
        name="unplane",
        stream=True,
        hold=parts[1:],
    )
    got = lax.all_to_all(pay, "z", 0, 0, tiled=True)
    results = {0: parts[0]}
    for s in SHIFTS:
        results[s] = shift(held[s - 1], s)
    (pay,) = call(
        place_body,
        "sv" + "a" * len(SHIFTS),
        [struct(MD, SUB, LOCAL)],
        [band_owner, got, *(results[s] for s in SHIFTS)],
        name="place",
        prefetch=True,
        stream=True,
    )
    (clip,) = call(norm_body, "v", [struct(1, LANES, dtype=F32)], [got], name="norm")
    placed = lax.all_to_all(pay, "m", 0, 0, tiled=True).reshape(ROW_DEV, LOCAL)
    update = (clip[0, 0] * placed.astype(F32)).astype(BF16)
    stat = struct(SLOTS, ROW_DEV, BLK, dtype=F32)
    new_left, new_right, new_moment = call(
        finish_body,
        "svv" + "v" * MD,
        [stat, stat, struct(SLOTS, ROW_DEV, BLK)],
        [source, left_stats[0], right_stats[0], *(results[s] for s in range(MD))],
        name="finish",
    )
    return update, new_second, new_left[None], new_right[None], new_moment[None]


def solution(mesh):
    owners, groups = mesh.devices.shape
    inner = Mesh(mesh.devices.reshape(owners // YDIM, YDIM, groups), AXES)
    wide = P(("z", "y"), "m")
    stats = P(("z", "y"), None, "m", None)
    return jax.shard_map(
        shards,
        mesh=inner,
        in_specs=(wide, wide, P(), stats, stats, stats, stats, stats),
        out_specs=(wide, wide, stats, stats, stats),
        check_vma=False,
    )
```

```python
import math

import jax
import jax.numpy as jnp
from jax import lax
from jax.experimental import pallas as pl
from jax.experimental.pallas import tpu as pltpu
from jax.sharding import Mesh
from jax.sharding import PartitionSpec as P

BLK = 512
ROWS = 4096
COLS = 16384
YDIM = 4
AXES = ("z", "y", "m")

ZD, MD = 16, 8
OWNERS = ZD * YDIM
BANDS = ROWS // BLK
CB = COLS // BLK
ZZ = ZD // BANDS
SUB = 8
ROW_DEV = 64
LOCAL = COLS // MD
LB = LOCAL // BLK
LANES = 128
TB = BLK // LANES
SLOTS = 4
AREA = BLK * BLK
SHIFTS = (4, 5, 3, 6, 2, 7, 1)
CHUNKS = 4

BF16, F32 = jnp.bfloat16, jnp.float32


def struct(*shape, dtype=BF16):
    return jax.ShapeDtypeStruct(shape, dtype)


def hold_shapes(hold):
    return [struct(*a.shape, dtype=a.dtype) for a in hold]


def call(
    body,
    specs,
    outs,
    args,
    scratch=(),
    vmem=16,
    flops=0,
    name=None,
    stream=False,
    hold=(),
    prefetch=False,
):
    space = {"v": pltpu.VMEM, "s": pltpu.SMEM, "a": pl.ANY}
    size = sum(o.size * o.dtype.itemsize for o in outs)
    size += sum(a.size * a.dtype.itemsize for a, k in zip(args, specs) if k == "v")
    first = len(args)
    specs, args, outs = specs + "a" * len(hold), [*args, *hold], [*outs, *hold_shapes(hold)]
    scratch = list(scratch)
    if stream:
        scratch += [pltpu.VMEM(outs[0].shape, outs[0].dtype), pltpu.SemaphoreType.DMA((CHUNKS + 1,))]
    count = specs.count("s") if prefetch else 0
    return pl.pallas_call(
        body,
        out_shape=tuple(outs),
        grid_spec=pltpu.PrefetchScalarGridSpec(
            num_scalar_prefetch=count,
            grid=(),
            in_specs=[pl.BlockSpec(memory_space=space[k]) for k in specs[count:]],
            out_specs=tuple(
                pl.BlockSpec(memory_space=space["a" if stream else "v"]) for _ in outs
            ),
            scratch_shapes=scratch,
        ),
        input_output_aliases={first + i: 1 + i for i in range(len(hold))},
        compiler_params=pltpu.CompilerParams(vmem_limit_bytes=vmem * 1024 * 1024),
        cost_estimate=pl.CostEstimate(flops=flops, bytes_accessed=size, transcendentals=0),
        name=name,
    )(*args)


def stream(fill, out, buffer, sems):
    size = buffer.shape[0] // CHUNKS
    copies = []
    for i in range(CHUNKS):
        for row in range(i * size, (i + 1) * size):
            fill(row)
        rows = pl.ds(i * size, size)
        copy = pltpu.make_async_copy(buffer.at[rows], out.at[rows], sems.at[i])
        copy.start()
        copies.append(copy)
    for copy in copies:
        copy.wait()


def join(first, second):
    return jnp.concatenate([first, second], axis=0)


def encode(value):
    value = jnp.broadcast_to(value, (SUB, LANES))
    row = lax.broadcasted_iota(jnp.int32, (SUB, LANES), 0)
    high = value.astype(BF16).astype(F32)
    mid = (value - high).astype(BF16).astype(F32)
    low = value - high - mid
    return jnp.where(
        row == 0, high, jnp.where(row == 1, mid, jnp.where(row == 2, low, 0.0))
    ).astype(BF16)


def decode(tile):
    return jnp.sum(tile.astype(F32), axis=0, keepdims=True)


def adam_body(index, grad, second, new_second, tile, sums):
    step = pl.program_id(0)

    @pl.when(step == 0)
    def _():
        sums[...] = jnp.zeros_like(sums)

    g = grad[...].astype(F32)
    ns = 0.999 * second[...] + 0.001 * g * g
    new_second[...] = ns
    d = g / (jnp.sqrt(ns) + 1e-08)
    q = d * d
    for c in range(LB * TB):
        cols = slice(c * LANES, (c + 1) * LANES)
        sums[c // TB] += q[:SUB, cols] + q[SUB:, cols]

    @pl.when(step == ROW_DEV // 16 - 1)
    def _():
        lane = lax.broadcasted_iota(jnp.int32, (1, LANES), 1)
        first = index[0] * LB
        value = jnp.zeros((1, LANES), F32)
        for j in range(LB):
            value = jnp.where(lane == first + j, jnp.sum(sums[j]), value)
        tile[...] = encode(value)


def adam(index, gradient, second_moment):
    rows = pl.BlockSpec((16, LOCAL), lambda i: (i, 0))
    return pl.pallas_call(
        adam_body,
        grid=(ROW_DEV // 16,),
        out_shape=(struct(ROW_DEV, LOCAL, dtype=F32), struct(SUB, LANES)),
        in_specs=[pl.BlockSpec(memory_space=pltpu.SMEM), rows, rows],
        out_specs=(rows, pl.BlockSpec((SUB, LANES), lambda i: (0, 0))),
        scratch_shapes=[pltpu.VMEM((LB, SUB, LANES), F32)],
        compiler_params=pltpu.CompilerParams(vmem_limit_bytes=16 * 1024 * 1024),
        name="adam",
    )(index, gradient, second_moment)


def spread_body(inverse, tile, got, before, out, buffer, sems):
    def fill(z):
        for y in range(YDIM):
            j = inverse[z * YDIM + y]
            lanes = pl.ds(pl.multiple_of((j & (LB - 1)) * BLK, BLK), BLK)
            piece = got[j >> 2, :, lanes]
            for c in range(TB):
                buffer[z, y * TB + c] = piece[:, c * LANES : (c + 1) * LANES]
        buffer[z, YDIM * TB] = tile[...]

    stream(fill, out, buffer, sems)


def pack_body(to, left, right, moment, after, *outs):
    for s in range(1, MD):
        t = to[s]
        outs[s - 1][0] = left[t]
        outs[s - 1][1] = right[t]
        outs[s - 1][2] = moment[t]


def plane_body(got, *refs):
    out, buffer, sems = refs[-3:]
    tiles = []
    for b in range(BANDS):
        total = decode(got[b * ZZ, YDIM * TB])
        for k in range(1, ZZ):
            total += decode(got[b * ZZ + k, YDIM * TB])
        tiles.append(encode(total))

    def fill(row):
        y, b = divmod(row, BANDS)
        for k in range(ZZ):
            buffer[row, k * TB : (k + 1) * TB] = got[b * ZZ + k, y * TB : (y + 1) * TB]
        buffer[row, ZZ * TB] = tiles[b]

    stream(fill, out, buffer, sems)


def roots_body(other, to, left, right, moment, *refs):
    parts, outs = refs[: MD - 1], refs[MD - 1 :]
    for s in range(MD):
        source = lax.rem(other[0] - s + MD, MD)
        rows = pl.ds(pl.multiple_of(source * ROW_DEV, ROW_DEV), ROW_DEV)
        for i, own in enumerate((left, right, moment)):
            outs[i][rows, :] = parts[s - 1][i] if s else own[to[0]]


def assemble(got, block):
    for k in range(ZZ):
        for y in range(YDIM):
            for g in range(0, MD, 2):
                row = (k * YDIM + y) * ROW_DEV + g * SUB
                for c in range(TB):
                    block[row : row + 16, c * LANES : (c + 1) * LANES] = join(
                        got[y * MD + g, k * TB + c], got[y * MD + g + 1, k * TB + c]
                    )


def block_body(masks, got, left, right, old, out, block, applied, prod, buffer, sems):
    assemble(got, block)
    adam = got[0, ZZ * TB].astype(F32)
    for i in range(1, YDIM * MD):
        adam += got[i, ZZ * TB].astype(F32)
    adam = jnp.sum(jnp.where(masks[:1, :] > 0, decode(adam), 0.0), keepdims=True)
    applied[...] = jnp.dot(left[...], block[...], preferred_element_type=F32).astype(BF16)
    p = jnp.dot(applied[...], right[...], preferred_element_type=F32)
    prod[...] = p
    norm = jnp.sum(p * p, keepdims=True)
    graft = jnp.sqrt(adam / AREA) / jnp.sqrt(norm / AREA + 1e-06)
    total = jnp.zeros((16, BLK), F32)
    copies = []
    for y in range(YDIM):
        for g in range(0, MD, 2):
            for k in range(ZZ):
                row = (k * YDIM + y) * ROW_DEV + g * SUB
                rows = slice(row, row + 16)
                f = 0.9 * old[rows, :].astype(F32) + graft * prod[rows, :]
                total += f * f
                for c in range(TB):
                    cols = slice(c * LANES, (c + 1) * LANES)
                    buffer[y * MD + g, k * TB + c] = f[:SUB, cols].astype(BF16)
                    buffer[y * MD + g + 1, k * TB + c] = f[SUB:, cols].astype(BF16)
        if y < YDIM - 1:
            part = (pl.ds(y * MD, MD), pl.ds(0, ZZ * TB))
            copies.append(pltpu.make_async_copy(buffer.at[part], out.at[part], sems.at[y]))
            copies[-1].start()
    square = jnp.broadcast_to(jnp.sum(total, keepdims=True), (1, LANES))
    tile = encode(jnp.where(masks[1:2, :] > 0, square, 0.0))
    for slot in range(YDIM * MD):
        buffer[slot, ZZ * TB] = tile
    last = (YDIM - 1) * MD
    rest = pl.ds(last, MD)
    copies.append(pltpu.make_async_copy(buffer.at[rest], out.at[rest], sems.at[YDIM - 1]))
    part = (pl.ds(0, last), pl.ds(ZZ * TB, 1))
    copies.append(pltpu.make_async_copy(buffer.at[part], out.at[part], sems.at[YDIM]))
    for copy in copies[-2:]:
        copy.start()
    for copy in copies:
        copy.wait()


def stats_body(other, got, moment, *refs):
    outs, (block, left, right) = refs[:MD], refs[MD:]
    assemble(got, block)
    left[...] = lax.dot_general(
        block[...], block[...], (((1,), (1,)), ((), ())), preferred_element_type=F32
    ).astype(BF16)
    right[...] = lax.dot_general(
        block[...], block[...], (((0,), (0,)), ((), ())), preferred_element_type=F32
    ).astype(BF16)
    for s, out in enumerate(outs):
        to = lax.rem(other[0] + s, MD)
        rows = pl.ds(pl.multiple_of(to * ROW_DEV, ROW_DEV), ROW_DEV)
        out[0] = left[rows, :]
        out[1] = right[rows, :]
        first, tiles = lax.rem(to, YDIM) * MD, (to // YDIM) * TB
        for g in range(0, MD, 2):
            for c in range(TB):
                out[2, g * SUB : g * SUB + 16, c * LANES : (c + 1) * LANES] = join(
                    moment[first + g, tiles + c], moment[first + g + 1, tiles + c]
                )


def unplane_body(got, *refs):
    out, (buffer, sems) = refs[MD - 1], refs[-2:]
    total = got[0, ZZ * TB].astype(F32)
    for i in range(1, YDIM * BANDS):
        total += got[i, ZZ * TB].astype(F32)
    tile = encode(decode(total))

    def fill(z):
        b, k = divmod(z, ZZ)
        for y in range(YDIM):
            buffer[z, y * TB : (y + 1) * TB] = got[y * BANDS + b, k * TB : (k + 1) * TB]
        buffer[z, YDIM * TB] = tile

    stream(fill, out, buffer, sems)


def place_body(band_owner, got, *refs):
    out, buffer, sems = refs[-3:]

    def fill(m):
        for i in range(LB):
            o = band_owner[m * LB + i]
            z, first = o >> 2, (o & (YDIM - 1)) * TB
            for c in range(TB):
                col = (i * TB + c) * LANES
                buffer[m, :, col : col + LANES] = got[z, first + c]

    stream(fill, out, buffer, sems)


def norm_body(got, out):
    total = got[0, YDIM * TB].astype(F32)
    for z in range(1, ZD):
        total += got[z, YDIM * TB].astype(F32)
    out[...] = jnp.minimum(1.0, 0.5 * math.sqrt(ROWS * COLS) / jnp.sqrt(decode(total)))


def finish_body(source, left, right, *refs):
    parts, (new_left, new_right, new_moment) = refs[:MD], refs[MD:]
    for s in range(MD):
        t = source[s]

        @pl.when(t >= 0)
        def _():
            new_left[t] = 0.95 * left[t] + 0.05 * parts[s][0].astype(F32)
            new_right[t] = 0.95 * right[t] + 0.05 * parts[s][1].astype(F32)
            new_moment[t] = parts[s][2]


def make_plan(owner_table):
    z = lax.axis_index("z")
    m = lax.axis_index("m")
    owner = z * YDIM + lax.axis_index("y")
    table = owner_table.reshape(BANDS, CB)
    band_owner = lax.dynamic_index_in_dim(table, z // ZZ, 0, keepdims=False)
    iota = lambda n: jnp.arange(n, dtype=jnp.int32)
    held = band_owner[None, :] == iota(OWNERS)[:, None]
    inverse = jnp.sum(jnp.where(held, iota(CB)[None, :], 0), axis=1)
    mine = table == owner
    has = jnp.sum(mine.astype(jnp.int32), axis=1)
    column = jnp.sum(jnp.where(mine, iota(CB)[None, :], 0), axis=1)
    slot = jnp.sum(jnp.where(iota(BANDS)[None, :] < iota(BANDS)[:, None], has[None, :], 0), axis=1)
    slot = jnp.minimum(slot, SLOTS - 1)
    pick = lambda at, values: jnp.sum(
        jnp.where(iota(BANDS)[None, :] == at[:, None], values[None, :], 0), axis=1
    )
    to = pick(lax.rem(m + iota(MD), MD), slot)
    source = pick(lax.rem(m - iota(MD) + MD, MD), jnp.where(has > 0, slot, -1))
    self = m[None]
    lane = jnp.where(iota(LANES) == pick(self, column), 1.0, 0.0)
    held = jnp.broadcast_to(pick(self, has), (LANES,)).astype(F32)
    masks = jnp.pad(jnp.stack([lane, held]), ((0, SUB - 2), (0, 0)))
    return inverse, band_owner, to, source, self, masks


def shift(part, s):
    return lax.ppermute(part, "m", [(i, (i + s) % MD) for i in range(MD)])


def shards(
    gradient, second_moment, owner_table, left_stats, right_stats, left_root, right_root, momentum
):
    inverse, band_owner, to, source, other, masks = make_plan(owner_table)
    square = (BLK, BLK)

    got = lax.all_to_all(gradient.reshape(MD, SUB, LOCAL), "m", 0, 0, tiled=True)
    new_second, tile = adam(lax.axis_index("m")[None], gradient, second_moment)
    (pay,) = call(
        spread_body,
        "svva",
        [struct(ZD, YDIM * TB + 1, SUB, LANES)],
        [inverse, tile, got, to],
        name="spread",
        prefetch=True,
        stream=True,
    )
    packed = call(
        pack_body,
        "svvva",
        [struct(3, ROW_DEV, BLK)] * (MD - 1),
        [to, left_root[0], right_root[0], momentum[0], pay],
        name="pack",
        prefetch=True,
    )
    got = lax.all_to_all(pay, "z", 0, 0, tiled=True)
    moved = {s: shift(packed[s - 1], s) for s in SHIFTS}
    (pay,) = call(
        plane_body,
        "v" + "a" * len(SHIFTS),
        [struct(YDIM * BANDS, ZZ * TB + 1, SUB, LANES)],
        [got, *(moved[s] for s in SHIFTS)],
        name="plane",
        stream=True,
    )
    got = lax.all_to_all(pay, ("y", "m"), 0, 0, tiled=True)
    left, right, old = call(
        roots_body,
        "ssvvv" + "v" * (MD - 1),
        [struct(*square)] * 3,
        [other, to, left_root[0], right_root[0], momentum[0], *(moved[s] for s in range(1, MD))],
        name="roots",
    )
    whole = got
    (back,) = call(
        block_body,
        "vvvvv",
        [struct(YDIM * MD, ZZ * TB + 1, SUB, LANES)],
        [masks, whole, left, right, old],
        scratch=[
            pltpu.VMEM(square, BF16),
            pltpu.VMEM(square, BF16),
            pltpu.VMEM(square, F32),
        ],
        flops=4 * BLK**3,
        vmem=24,
        name="block",
        stream=True,
    )
    got = lax.all_to_all(back, ("y", "m"), 0, 0, tiled=True)
    parts = call(
        stats_body,
        "svv",
        [struct(3, ROW_DEV, BLK)] * MD,
        [other, whole, back],
        scratch=[pltpu.VMEM(square, BF16)] * 3,
        flops=4 * BLK**3,
        name="stats",
    )
    pay, *held = call(
        unplane_body,
        "v",
        [struct(ZD, YDIM * TB + 1, SUB, LANES)],
        [got],
        name="unplane",
        stream=True,
        hold=parts[1:],
    )
    got = lax.all_to_all(pay, "z", 0, 0, tiled=True)
    results = {0: parts[0]}
    for s in SHIFTS:
        results[s] = shift(held[s - 1], s)
    (pay,) = call(
        place_body,
        "sv" + "a" * len(SHIFTS),
        [struct(MD, SUB, LOCAL)],
        [band_owner, got, *(results[s] for s in SHIFTS)],
        name="place",
        prefetch=True,
        stream=True,
    )
    (clip,) = call(norm_body, "v", [struct(1, LANES, dtype=F32)], [got], name="norm")
    placed = lax.all_to_all(pay, "m", 0, 0, tiled=True).reshape(ROW_DEV, LOCAL)
    update = (clip[0, 0] * placed.astype(F32)).astype(BF16)
    stat = struct(SLOTS, ROW_DEV, BLK, dtype=F32)
    new_left, new_right, new_moment = call(
        finish_body,
        "svv" + "v" * MD,
        [stat, stat, struct(SLOTS, ROW_DEV, BLK)],
        [source, left_stats[0], right_stats[0], *(results[s] for s in range(MD))],
        name="finish",
    )
    return update, new_second, new_left[None], new_right[None], new_moment[None]


def solution(mesh):
    owners, groups = mesh.devices.shape
    inner = Mesh(mesh.devices.reshape(owners // YDIM, YDIM, groups), AXES)
    wide = P(("z", "y"), "m")
    stats = P(("z", "y"), None, "m", None)
    return jax.shard_map(
        shards,
        mesh=inner,
        in_specs=(wide, wide, P(), stats, stats, stats, stats, stats),
        out_specs=(wide, wide, stats, stats, stats),
        check_vma=False,
    )
```

```python
import math

import jax
import jax.numpy as jnp
from jax import lax
from jax.experimental import pallas as pl
from jax.experimental.pallas import tpu as pltpu
from jax.sharding import Mesh
from jax.sharding import PartitionSpec as P

BLK = 512
ROWS = 4096
COLS = 16384
YDIM = 4
AXES = ("z", "y", "m")

ZD, MD = 16, 8
OWNERS = ZD * YDIM
BANDS = ROWS // BLK
CB = COLS // BLK
ZZ = ZD // BANDS
SUB = 8
ROW_DEV = 64
LOCAL = COLS // MD
LB = LOCAL // BLK
LANES = 128
TB = BLK // LANES
SLOTS = 4
AREA = BLK * BLK
SHIFTS = (4, 5, 3, 6, 2, 7, 1)
CHUNKS = 4

BF16, F32 = jnp.bfloat16, jnp.float32


def struct(*shape, dtype=BF16):
    return jax.ShapeDtypeStruct(shape, dtype)


def hold_shapes(hold):
    return [struct(*a.shape, dtype=a.dtype) for a in hold]


def call(
    body,
    specs,
    outs,
    args,
    scratch=(),
    vmem=16,
    flops=0,
    name=None,
    stream=False,
    hold=(),
    prefetch=False,
):
    space = {"v": pltpu.VMEM, "s": pltpu.SMEM, "a": pl.ANY}
    size = sum(o.size * o.dtype.itemsize for o in outs)
    size += sum(a.size * a.dtype.itemsize for a, k in zip(args, specs) if k == "v")
    first = len(args)
    specs, args, outs = specs + "a" * len(hold), [*args, *hold], [*outs, *hold_shapes(hold)]
    scratch = list(scratch)
    if stream:
        scratch += [pltpu.VMEM(outs[0].shape, outs[0].dtype), pltpu.SemaphoreType.DMA((CHUNKS + 1,))]
    count = specs.count("s") if prefetch else 0
    return pl.pallas_call(
        body,
        out_shape=tuple(outs),
        grid_spec=pltpu.PrefetchScalarGridSpec(
            num_scalar_prefetch=count,
            grid=(),
            in_specs=[pl.BlockSpec(memory_space=space[k]) for k in specs[count:]],
            out_specs=tuple(
                pl.BlockSpec(memory_space=space["a" if stream else "v"]) for _ in outs
            ),
            scratch_shapes=scratch,
        ),
        input_output_aliases={first + i: 1 + i for i in range(len(hold))},
        compiler_params=pltpu.CompilerParams(vmem_limit_bytes=vmem * 1024 * 1024),
        cost_estimate=pl.CostEstimate(flops=flops, bytes_accessed=size, transcendentals=0),
        name=name,
    )(*args)


def stream(fill, out, buffer, sems):
    size = buffer.shape[0] // CHUNKS
    copies = []
    for i in range(CHUNKS):
        for row in range(i * size, (i + 1) * size):
            fill(row)
        rows = pl.ds(i * size, size)
        copy = pltpu.make_async_copy(buffer.at[rows], out.at[rows], sems.at[i])
        copy.start()
        copies.append(copy)
    for copy in copies:
        copy.wait()


def join(first, second):
    return jnp.concatenate([first, second], axis=0)


def encode(value):
    value = jnp.broadcast_to(value, (SUB, LANES))
    row = lax.broadcasted_iota(jnp.int32, (SUB, LANES), 0)
    high = value.astype(BF16).astype(F32)
    mid = (value - high).astype(BF16).astype(F32)
    low = value - high - mid
    return jnp.where(
        row == 0, high, jnp.where(row == 1, mid, jnp.where(row == 2, low, 0.0))
    ).astype(BF16)


def decode(tile):
    return jnp.sum(tile.astype(F32), axis=0, keepdims=True)


def adam_body(index, grad, second, new_second, tile, sums):
    step = pl.program_id(0)

    @pl.when(step == 0)
    def _():
        sums[...] = jnp.zeros_like(sums)

    g = grad[...].astype(F32)
    ns = 0.999 * second[...] + 0.001 * g * g
    new_second[...] = ns
    d = g / (jnp.sqrt(ns) + 1e-08)
    q = d * d
    for c in range(LB * TB):
        cols = slice(c * LANES, (c + 1) * LANES)
        sums[c // TB] += q[:SUB, cols] + q[SUB:, cols]

    @pl.when(step == ROW_DEV // 16 - 1)
    def _():
        lane = lax.broadcasted_iota(jnp.int32, (1, LANES), 1)
        first = index[0] * LB
        value = jnp.zeros((1, LANES), F32)
        for j in range(LB):
            value = jnp.where(lane == first + j, jnp.sum(sums[j]), value)
        tile[...] = encode(value)


def adam(index, gradient, second_moment):
    rows = pl.BlockSpec((16, LOCAL), lambda i: (i, 0))
    return pl.pallas_call(
        adam_body,
        grid=(ROW_DEV // 16,),
        out_shape=(struct(ROW_DEV, LOCAL, dtype=F32), struct(SUB, LANES)),
        in_specs=[pl.BlockSpec(memory_space=pltpu.SMEM), rows, rows],
        out_specs=(rows, pl.BlockSpec((SUB, LANES), lambda i: (0, 0))),
        scratch_shapes=[pltpu.VMEM((LB, SUB, LANES), F32)],
        compiler_params=pltpu.CompilerParams(vmem_limit_bytes=16 * 1024 * 1024),
        name="adam",
    )(index, gradient, second_moment)


def spread_body(inverse, tile, got, before, out, buffer, sems):
    def fill(z):
        for y in range(YDIM):
            j = inverse[z * YDIM + y]
            lanes = pl.ds(pl.multiple_of((j & (LB - 1)) * BLK, BLK), BLK)
            piece = got[j >> 2, :, lanes]
            for c in range(TB):
                buffer[z, y * TB + c] = piece[:, c * LANES : (c + 1) * LANES]
        buffer[z, YDIM * TB] = tile[...]

    stream(fill, out, buffer, sems)


def pack_body(to, left, right, moment, after, *outs):
    for s in range(1, MD):
        t = to[s]
        outs[s - 1][0] = left[t]
        outs[s - 1][1] = right[t]
        outs[s - 1][2] = moment[t]


def plane_body(got, *refs):
    out, buffer, sems = refs[-3:]
    tiles = []
    for b in range(BANDS):
        total = decode(got[b * ZZ, YDIM * TB])
        for k in range(1, ZZ):
            total += decode(got[b * ZZ + k, YDIM * TB])
        tiles.append(encode(total))

    def fill(row):
        y, b = divmod(row, BANDS)
        for k in range(ZZ):
            buffer[row, k * TB : (k + 1) * TB] = got[b * ZZ + k, y * TB : (y + 1) * TB]
        buffer[row, ZZ * TB] = tiles[b]

    stream(fill, out, buffer, sems)


def roots_body(other, to, left, right, moment, *refs):
    parts, outs, sems = refs[: MD - 1], refs[MD - 1 : -1], refs[-1]
    copies = []
    for s in range(MD):
        source = lax.rem(other[0] - s + MD, MD)
        rows = pl.ds(pl.multiple_of(source * ROW_DEV, ROW_DEV), ROW_DEV)
        for i, own in enumerate((left, right, moment)):
            if s:
                outs[i][rows, :] = parts[s - 1][i]
            else:
                copies.append(pltpu.make_async_copy(own.at[to[0]], outs[i].at[rows], sems.at[i]))
                copies[-1].start()
    for copy in copies:
        copy.wait()


def assemble(got, block):
    for k in range(ZZ):
        for y in range(YDIM):
            for g in range(0, MD, 2):
                row = (k * YDIM + y) * ROW_DEV + g * SUB
                for c in range(TB):
                    block[row : row + 16, c * LANES : (c + 1) * LANES] = join(
                        got[y * MD + g, k * TB + c], got[y * MD + g + 1, k * TB + c]
                    )


def block_body(
    masks, got, left, right_in, old_in, out, block, applied, prod, right, old, fetch, buffer, sems
):
    fetches = [
        pltpu.make_async_copy(right_in, right, fetch.at[0]),
        pltpu.make_async_copy(old_in, old, fetch.at[1]),
    ]
    for copy in fetches:
        copy.start()
    assemble(got, block)
    adam = got[0, ZZ * TB].astype(F32)
    for i in range(1, YDIM * MD):
        adam += got[i, ZZ * TB].astype(F32)
    adam = jnp.sum(jnp.where(masks[:1, :] > 0, decode(adam), 0.0), keepdims=True)
    applied[...] = jnp.dot(left[...], block[...], preferred_element_type=F32).astype(BF16)
    for copy in fetches:
        copy.wait()
    p = jnp.dot(applied[...], right[...], preferred_element_type=F32)
    prod[...] = p
    norm = jnp.sum(p * p, keepdims=True)
    graft = jnp.sqrt(adam / AREA) / jnp.sqrt(norm / AREA + 1e-06)
    total = jnp.zeros((16, BLK), F32)
    copies = []
    for y in range(YDIM):
        for g in range(0, MD, 2):
            for k in range(ZZ):
                row = (k * YDIM + y) * ROW_DEV + g * SUB
                rows = slice(row, row + 16)
                f = 0.9 * old[rows, :].astype(F32) + graft * prod[rows, :]
                total += f * f
                for c in range(TB):
                    cols = slice(c * LANES, (c + 1) * LANES)
                    buffer[y * MD + g, k * TB + c] = f[:SUB, cols].astype(BF16)
                    buffer[y * MD + g + 1, k * TB + c] = f[SUB:, cols].astype(BF16)
        if y < YDIM - 1:
            part = (pl.ds(y * MD, MD), pl.ds(0, ZZ * TB))
            copies.append(pltpu.make_async_copy(buffer.at[part], out.at[part], sems.at[y]))
            copies[-1].start()
    square = jnp.broadcast_to(jnp.sum(total, keepdims=True), (1, LANES))
    tile = encode(jnp.where(masks[1:2, :] > 0, square, 0.0))
    for slot in range(YDIM * MD):
        buffer[slot, ZZ * TB] = tile
    last = (YDIM - 1) * MD
    rest = pl.ds(last, MD)
    copies.append(pltpu.make_async_copy(buffer.at[rest], out.at[rest], sems.at[YDIM - 1]))
    part = (pl.ds(0, last), pl.ds(ZZ * TB, 1))
    copies.append(pltpu.make_async_copy(buffer.at[part], out.at[part], sems.at[YDIM]))
    for copy in copies[-2:]:
        copy.start()
    for copy in copies:
        copy.wait()


def stats_body(other, got, moment, *refs):
    outs, (block, left, right) = refs[:MD], refs[MD:]
    assemble(got, block)
    left[...] = lax.dot_general(
        block[...], block[...], (((1,), (1,)), ((), ())), preferred_element_type=F32
    ).astype(BF16)
    right[...] = lax.dot_general(
        block[...], block[...], (((0,), (0,)), ((), ())), preferred_element_type=F32
    ).astype(BF16)
    for s, out in enumerate(outs):
        to = lax.rem(other[0] + s, MD)
        rows = pl.ds(pl.multiple_of(to * ROW_DEV, ROW_DEV), ROW_DEV)
        out[0] = left[rows, :]
        out[1] = right[rows, :]
        first, tiles = lax.rem(to, YDIM) * MD, (to // YDIM) * TB
        for g in range(0, MD, 2):
            for c in range(TB):
                out[2, g * SUB : g * SUB + 16, c * LANES : (c + 1) * LANES] = join(
                    moment[first + g, tiles + c], moment[first + g + 1, tiles + c]
                )


def unplane_body(got, *refs):
    out, (buffer, sems) = refs[MD - 1], refs[-2:]
    total = got[0, ZZ * TB].astype(F32)
    for i in range(1, YDIM * BANDS):
        total += got[i, ZZ * TB].astype(F32)
    tile = encode(decode(total))

    def fill(z):
        b, k = divmod(z, ZZ)
        for y in range(YDIM):
            buffer[z, y * TB : (y + 1) * TB] = got[y * BANDS + b, k * TB : (k + 1) * TB]
        buffer[z, YDIM * TB] = tile

    stream(fill, out, buffer, sems)


def place_body(band_owner, got, *refs):
    out, buffer, sems = refs[-3:]

    def fill(m):
        for i in range(LB):
            o = band_owner[m * LB + i]
            z, first = o >> 2, (o & (YDIM - 1)) * TB
            for c in range(TB):
                col = (i * TB + c) * LANES
                buffer[m, :, col : col + LANES] = got[z, first + c]

    stream(fill, out, buffer, sems)


def norm_body(got, out):
    total = got[0, YDIM * TB].astype(F32)
    for z in range(1, ZD):
        total += got[z, YDIM * TB].astype(F32)
    out[...] = jnp.minimum(1.0, 0.5 * math.sqrt(ROWS * COLS) / jnp.sqrt(decode(total)))


def finish_body(source, left, right, *refs):
    parts, (new_left, new_right, new_moment) = refs[:MD], refs[MD:]
    for s in range(MD):
        t = source[s]

        @pl.when(t >= 0)
        def _():
            new_left[t] = 0.95 * left[t] + 0.05 * parts[s][0].astype(F32)
            new_right[t] = 0.95 * right[t] + 0.05 * parts[s][1].astype(F32)
            new_moment[t] = parts[s][2]


def make_plan(owner_table):
    z = lax.axis_index("z")
    m = lax.axis_index("m")
    owner = z * YDIM + lax.axis_index("y")
    table = owner_table.reshape(BANDS, CB)
    band_owner = lax.dynamic_index_in_dim(table, z // ZZ, 0, keepdims=False)
    iota = lambda n: jnp.arange(n, dtype=jnp.int32)
    held = band_owner[None, :] == iota(OWNERS)[:, None]
    inverse = jnp.sum(jnp.where(held, iota(CB)[None, :], 0), axis=1)
    mine = table == owner
    has = jnp.sum(mine.astype(jnp.int32), axis=1)
    column = jnp.sum(jnp.where(mine, iota(CB)[None, :], 0), axis=1)
    slot = jnp.sum(jnp.where(iota(BANDS)[None, :] < iota(BANDS)[:, None], has[None, :], 0), axis=1)
    slot = jnp.minimum(slot, SLOTS - 1)
    pick = lambda at, values: jnp.sum(
        jnp.where(iota(BANDS)[None, :] == at[:, None], values[None, :], 0), axis=1
    )
    to = pick(lax.rem(m + iota(MD), MD), slot)
    source = pick(lax.rem(m - iota(MD) + MD, MD), jnp.where(has > 0, slot, -1))
    self = m[None]
    lane = jnp.where(iota(LANES) == pick(self, column), 1.0, 0.0)
    held = jnp.broadcast_to(pick(self, has), (LANES,)).astype(F32)
    masks = jnp.pad(jnp.stack([lane, held]), ((0, SUB - 2), (0, 0)))
    return inverse, band_owner, to, source, self, masks


def shift(part, s):
    return lax.ppermute(part, "m", [(i, (i + s) % MD) for i in range(MD)])


def shards(
    gradient, second_moment, owner_table, left_stats, right_stats, left_root, right_root, momentum
):
    inverse, band_owner, to, source, other, masks = make_plan(owner_table)
    square = (BLK, BLK)

    got = lax.all_to_all(gradient.reshape(MD, SUB, LOCAL), "m", 0, 0, tiled=True)
    new_second, tile = adam(lax.axis_index("m")[None], gradient, second_moment)
    (pay,) = call(
        spread_body,
        "svva",
        [struct(ZD, YDIM * TB + 1, SUB, LANES)],
        [inverse, tile, got, to],
        name="spread",
        prefetch=True,
        stream=True,
    )
    packed = call(
        pack_body,
        "svvva",
        [struct(3, ROW_DEV, BLK)] * (MD - 1),
        [to, left_root[0], right_root[0], momentum[0], pay],
        name="pack",
        prefetch=True,
    )
    got = lax.all_to_all(pay, "z", 0, 0, tiled=True)
    moved = {s: shift(packed[s - 1], s) for s in SHIFTS}
    (pay,) = call(
        plane_body,
        "v" + "a" * len(SHIFTS),
        [struct(YDIM * BANDS, ZZ * TB + 1, SUB, LANES)],
        [got, *(moved[s] for s in SHIFTS)],
        name="plane",
        stream=True,
    )
    got = lax.all_to_all(pay, ("y", "m"), 0, 0, tiled=True)
    left, right, old = call(
        roots_body,
        "ssaaa" + "v" * (MD - 1),
        [struct(*square)] * 3,
        [other, to, left_root[0], right_root[0], momentum[0], *(moved[s] for s in range(1, MD))],
        scratch=[pltpu.SemaphoreType.DMA((3,))],
        name="roots",
    )
    whole = got
    (back,) = call(
        block_body,
        "vvvaa",
        [struct(YDIM * MD, ZZ * TB + 1, SUB, LANES)],
        [masks, whole, left, right, old],
        scratch=[
            pltpu.VMEM(square, BF16),
            pltpu.VMEM(square, BF16),
            pltpu.VMEM(square, F32),
            pltpu.VMEM(square, BF16),
            pltpu.VMEM(square, BF16),
            pltpu.SemaphoreType.DMA((2,)),
        ],
        flops=4 * BLK**3,
        vmem=24,
        name="block",
        stream=True,
    )
    got = lax.all_to_all(back, ("y", "m"), 0, 0, tiled=True)
    parts = call(
        stats_body,
        "svv",
        [struct(3, ROW_DEV, BLK)] * MD,
        [other, whole, back],
        scratch=[pltpu.VMEM(square, BF16)] * 3,
        flops=4 * BLK**3,
        name="stats",
    )
    pay, *held = call(
        unplane_body,
        "v",
        [struct(ZD, YDIM * TB + 1, SUB, LANES)],
        [got],
        name="unplane",
        stream=True,
        hold=parts[1:],
    )
    got = lax.all_to_all(pay, "z", 0, 0, tiled=True)
    results = {0: parts[0]}
    for s in SHIFTS:
        results[s] = shift(held[s - 1], s)
    (pay,) = call(
        place_body,
        "sv" + "a" * len(SHIFTS),
        [struct(MD, SUB, LOCAL)],
        [band_owner, got, *(results[s] for s in SHIFTS)],
        name="place",
        prefetch=True,
        stream=True,
    )
    (clip,) = call(norm_body, "v", [struct(1, LANES, dtype=F32)], [got], name="norm")
    placed = lax.all_to_all(pay, "m", 0, 0, tiled=True).reshape(ROW_DEV, LOCAL)
    update = (clip[0, 0] * placed.astype(F32)).astype(BF16)
    stat = struct(SLOTS, ROW_DEV, BLK, dtype=F32)
    new_left, new_right, new_moment = call(
        finish_body,
        "svv" + "v" * MD,
        [stat, stat, struct(SLOTS, ROW_DEV, BLK)],
        [source, left_stats[0], right_stats[0], *(results[s] for s in range(MD))],
        name="finish",
    )
    return update, new_second, new_left[None], new_right[None], new_moment[None]


def solution(mesh):
    owners, groups = mesh.devices.shape
    inner = Mesh(mesh.devices.reshape(owners // YDIM, YDIM, groups), AXES)
    wide = P(("z", "y"), "m")
    stats = P(("z", "y"), None, "m", None)
    return jax.shard_map(
        shards,
        mesh=inner,
        in_specs=(wide, wide, P(), stats, stats, stats, stats, stats),
        out_specs=(wide, wide, stats, stats, stats),
        check_vma=False,
    )
```

```python
import math

import jax
import jax.numpy as jnp
from jax import lax
from jax.experimental import pallas as pl
from jax.experimental.pallas import tpu as pltpu
from jax.sharding import Mesh
from jax.sharding import PartitionSpec as P

BLK = 512
ROWS = 4096
COLS = 16384
YDIM = 4
AXES = ("z", "y", "m")

ZD, MD = 16, 8
OWNERS = ZD * YDIM
BANDS = ROWS // BLK
CB = COLS // BLK
ZZ = ZD // BANDS
SUB = 8
ROW_DEV = 64
LOCAL = COLS // MD
LB = LOCAL // BLK
LANES = 128
TB = BLK // LANES
SLOTS = 4
AREA = BLK * BLK
SHIFTS = (2, 6, 4, 5, 3, 7, 1)
CHUNKS = 4

BF16, F32 = jnp.bfloat16, jnp.float32


def struct(*shape, dtype=BF16):
    return jax.ShapeDtypeStruct(shape, dtype)


def hold_shapes(hold):
    return [struct(*a.shape, dtype=a.dtype) for a in hold]


def call(
    body,
    specs,
    outs,
    args,
    scratch=(),
    vmem=16,
    flops=0,
    name=None,
    stream=False,
    hold=(),
    prefetch=False,
):
    space = {"v": pltpu.VMEM, "s": pltpu.SMEM, "a": pl.ANY}
    size = sum(o.size * o.dtype.itemsize for o in outs)
    size += sum(a.size * a.dtype.itemsize for a, k in zip(args, specs) if k == "v")
    first = len(args)
    specs, args, outs = specs + "a" * len(hold), [*args, *hold], [*outs, *hold_shapes(hold)]
    scratch = list(scratch)
    if stream:
        scratch += [pltpu.VMEM(outs[0].shape, outs[0].dtype), pltpu.SemaphoreType.DMA((CHUNKS + 1,))]
    count = specs.count("s") if prefetch else 0
    return pl.pallas_call(
        body,
        out_shape=tuple(outs),
        grid_spec=pltpu.PrefetchScalarGridSpec(
            num_scalar_prefetch=count,
            grid=(),
            in_specs=[pl.BlockSpec(memory_space=space[k]) for k in specs[count:]],
            out_specs=tuple(
                pl.BlockSpec(memory_space=space["a" if stream else "v"]) for _ in outs
            ),
            scratch_shapes=scratch,
        ),
        input_output_aliases={first + i: 1 + i for i in range(len(hold))},
        compiler_params=pltpu.CompilerParams(vmem_limit_bytes=vmem * 1024 * 1024),
        cost_estimate=pl.CostEstimate(flops=flops, bytes_accessed=size, transcendentals=0),
        name=name,
    )(*args)


def stream(fill, out, buffer, sems):
    size = buffer.shape[0] // CHUNKS
    copies = []
    for i in range(CHUNKS):
        for row in range(i * size, (i + 1) * size):
            fill(row)
        rows = pl.ds(i * size, size)
        copy = pltpu.make_async_copy(buffer.at[rows], out.at[rows], sems.at[i])
        copy.start()
        copies.append(copy)
    for copy in copies:
        copy.wait()


def join(first, second):
    return jnp.concatenate([first, second], axis=0)


def encode(value):
    value = jnp.broadcast_to(value, (SUB, LANES))
    row = lax.broadcasted_iota(jnp.int32, (SUB, LANES), 0)
    high = value.astype(BF16).astype(F32)
    mid = (value - high).astype(BF16).astype(F32)
    low = value - high - mid
    return jnp.where(
        row == 0, high, jnp.where(row == 1, mid, jnp.where(row == 2, low, 0.0))
    ).astype(BF16)


def decode(tile):
    return jnp.sum(tile.astype(F32), axis=0, keepdims=True)


def adam_body(index, grad, second, new_second, tile, sums):
    step = pl.program_id(0)

    @pl.when(step == 0)
    def _():
        sums[...] = jnp.zeros_like(sums)

    g = grad[...].astype(F32)
    ns = 0.999 * second[...] + 0.001 * g * g
    new_second[...] = ns
    d = g / (jnp.sqrt(ns) + 1e-08)
    q = d * d
    for c in range(LB * TB):
        cols = slice(c * LANES, (c + 1) * LANES)
        sums[c // TB] += q[:SUB, cols] + q[SUB:, cols]

    @pl.when(step == ROW_DEV // 16 - 1)
    def _():
        lane = lax.broadcasted_iota(jnp.int32, (1, LANES), 1)
        first = index[0] * LB
        value = jnp.zeros((1, LANES), F32)
        for j in range(LB):
            value = jnp.where(lane == first + j, jnp.sum(sums[j]), value)
        tile[...] = encode(value)


def adam(index, gradient, second_moment):
    rows = pl.BlockSpec((16, LOCAL), lambda i: (i, 0))
    return pl.pallas_call(
        adam_body,
        grid=(ROW_DEV // 16,),
        out_shape=(struct(ROW_DEV, LOCAL, dtype=F32), struct(SUB, LANES)),
        in_specs=[pl.BlockSpec(memory_space=pltpu.SMEM), rows, rows],
        out_specs=(rows, pl.BlockSpec((SUB, LANES), lambda i: (0, 0))),
        scratch_shapes=[pltpu.VMEM((LB, SUB, LANES), F32)],
        compiler_params=pltpu.CompilerParams(vmem_limit_bytes=16 * 1024 * 1024),
        name="adam",
    )(index, gradient, second_moment)


def spread_body(inverse, tile, got, before, out, buffer, sems):
    def fill(z):
        for y in range(YDIM):
            j = inverse[z * YDIM + y]
            lanes = pl.ds(pl.multiple_of((j & (LB - 1)) * BLK, BLK), BLK)
            piece = got[j >> 2, :, lanes]
            for c in range(TB):
                buffer[z, y * TB + c] = piece[:, c * LANES : (c + 1) * LANES]
        buffer[z, YDIM * TB] = tile[...]

    stream(fill, out, buffer, sems)


def pack_body(to, left, right, moment, after, *outs):
    for s in range(MD):
        t = to[s]
        outs[s][0] = left[t]
        outs[s][1] = right[t]
        outs[s][2] = moment[t]


def plane_body(got, *refs):
    out, buffer, sems = refs[-3:]
    tiles = []
    for b in range(BANDS):
        total = decode(got[b * ZZ, YDIM * TB])
        for k in range(1, ZZ):
            total += decode(got[b * ZZ + k, YDIM * TB])
        tiles.append(encode(total))

    def fill(row):
        y, b = divmod(row, BANDS)
        for k in range(ZZ):
            buffer[row, k * TB : (k + 1) * TB] = got[b * ZZ + k, y * TB : (y + 1) * TB]
        buffer[row, ZZ * TB] = tiles[b]

    stream(fill, out, buffer, sems)


def roots_body(other, *refs):
    parts, outs = refs[:MD], refs[MD:]
    for s in range(MD):
        source = lax.rem(other[0] - s + MD, MD)
        rows = pl.ds(pl.multiple_of(source * ROW_DEV, ROW_DEV), ROW_DEV)
        for i in range(3):
            outs[i][rows, :] = parts[s][i]


def assemble(got, block):
    for k in range(ZZ):
        for y in range(YDIM):
            for g in range(0, MD, 2):
                row = (k * YDIM + y) * ROW_DEV + g * SUB
                for c in range(TB):
                    block[row : row + 16, c * LANES : (c + 1) * LANES] = join(
                        got[y * MD + g, k * TB + c], got[y * MD + g + 1, k * TB + c]
                    )


def block_body(masks, got, left, right, old, out, block, applied, prod, buffer, sems):
    assemble(got, block)
    adam = got[0, ZZ * TB].astype(F32)
    for i in range(1, YDIM * MD):
        adam += got[i, ZZ * TB].astype(F32)
    adam = jnp.sum(jnp.where(masks[:1, :] > 0, decode(adam), 0.0), keepdims=True)
    applied[...] = jnp.dot(left[...], block[...], preferred_element_type=F32).astype(BF16)
    p = jnp.dot(applied[...], right[...], preferred_element_type=F32)
    prod[...] = p
    norm = jnp.sum(p * p, keepdims=True)
    graft = jnp.sqrt(adam / AREA) / jnp.sqrt(norm / AREA + 1e-06)
    total = jnp.zeros((16, BLK), F32)
    copies = []
    for y in range(YDIM):
        for g in range(0, MD, 2):
            for k in range(ZZ):
                row = (k * YDIM + y) * ROW_DEV + g * SUB
                rows = slice(row, row + 16)
                f = 0.9 * old[rows, :].astype(F32) + graft * prod[rows, :]
                total += f * f
                for c in range(TB):
                    cols = slice(c * LANES, (c + 1) * LANES)
                    buffer[y * MD + g, k * TB + c] = f[:SUB, cols].astype(BF16)
                    buffer[y * MD + g + 1, k * TB + c] = f[SUB:, cols].astype(BF16)
        if y < YDIM - 1:
            part = (pl.ds(y * MD, MD), pl.ds(0, ZZ * TB))
            copies.append(pltpu.make_async_copy(buffer.at[part], out.at[part], sems.at[y]))
            copies[-1].start()
    square = jnp.broadcast_to(jnp.sum(total, keepdims=True), (1, LANES))
    tile = encode(jnp.where(masks[1:2, :] > 0, square, 0.0))
    for slot in range(YDIM * MD):
        buffer[slot, ZZ * TB] = tile
    last = (YDIM - 1) * MD
    rest = pl.ds(last, MD)
    copies.append(pltpu.make_async_copy(buffer.at[rest], out.at[rest], sems.at[YDIM - 1]))
    part = (pl.ds(0, last), pl.ds(ZZ * TB, 1))
    copies.append(pltpu.make_async_copy(buffer.at[part], out.at[part], sems.at[YDIM]))
    for copy in copies[-2:]:
        copy.start()
    for copy in copies:
        copy.wait()


def stats_body(other, got, moment, *refs):
    outs, (block, left, right) = refs[:MD], refs[MD:]
    assemble(got, block)
    left[...] = lax.dot_general(
        block[...], block[...], (((1,), (1,)), ((), ())), preferred_element_type=F32
    ).astype(BF16)
    right[...] = lax.dot_general(
        block[...], block[...], (((0,), (0,)), ((), ())), preferred_element_type=F32
    ).astype(BF16)
    for s, out in enumerate(outs):
        to = lax.rem(other[0] + s, MD)
        rows = pl.ds(pl.multiple_of(to * ROW_DEV, ROW_DEV), ROW_DEV)
        out[0] = left[rows, :]
        out[1] = right[rows, :]
        first, tiles = lax.rem(to, YDIM) * MD, (to // YDIM) * TB
        for g in range(0, MD, 2):
            for c in range(TB):
                out[2, g * SUB : g * SUB + 16, c * LANES : (c + 1) * LANES] = join(
                    moment[first + g, tiles + c], moment[first + g + 1, tiles + c]
                )


def unplane_body(got, *refs):
    out, (buffer, sems) = refs[MD - 1], refs[-2:]
    total = got[0, ZZ * TB].astype(F32)
    for i in range(1, YDIM * BANDS):
        total += got[i, ZZ * TB].astype(F32)
    tile = encode(decode(total))

    def fill(z):
        b, k = divmod(z, ZZ)
        for y in range(YDIM):
            buffer[z, y * TB : (y + 1) * TB] = got[y * BANDS + b, k * TB : (k + 1) * TB]
        buffer[z, YDIM * TB] = tile

    stream(fill, out, buffer, sems)


def place_body(band_owner, got, *refs):
    out, buffer, sems = refs[-3:]

    def fill(m):
        for i in range(LB):
            o = band_owner[m * LB + i]
            z, first = o >> 2, (o & (YDIM - 1)) * TB
            for c in range(TB):
                col = (i * TB + c) * LANES
                buffer[m, :, col : col + LANES] = got[z, first + c]

    stream(fill, out, buffer, sems)


def norm_body(got, out):
    total = got[0, YDIM * TB].astype(F32)
    for z in range(1, ZD):
        total += got[z, YDIM * TB].astype(F32)
    out[...] = jnp.minimum(1.0, 0.5 * math.sqrt(ROWS * COLS) / jnp.sqrt(decode(total)))


def finish_body(source, left, right, *refs):
    parts, (new_left, new_right, new_moment) = refs[:MD], refs[MD:]
    for s in range(MD):
        t = source[s]

        @pl.when(t >= 0)
        def _():
            new_left[t] = 0.95 * left[t] + 0.05 * parts[s][0].astype(F32)
            new_right[t] = 0.95 * right[t] + 0.05 * parts[s][1].astype(F32)
            new_moment[t] = parts[s][2]


def make_plan(owner_table):
    z = lax.axis_index("z")
    m = lax.axis_index("m")
    owner = z * YDIM + lax.axis_index("y")
    table = owner_table.reshape(BANDS, CB)
    band_owner = lax.dynamic_index_in_dim(table, z // ZZ, 0, keepdims=False)
    iota = lambda n: jnp.arange(n, dtype=jnp.int32)
    held = band_owner[None, :] == iota(OWNERS)[:, None]
    inverse = jnp.sum(jnp.where(held, iota(CB)[None, :], 0), axis=1)
    mine = table == owner
    has = jnp.sum(mine.astype(jnp.int32), axis=1)
    column = jnp.sum(jnp.where(mine, iota(CB)[None, :], 0), axis=1)
    slot = jnp.sum(jnp.where(iota(BANDS)[None, :] < iota(BANDS)[:, None], has[None, :], 0), axis=1)
    slot = jnp.minimum(slot, SLOTS - 1)
    pick = lambda at, values: jnp.sum(
        jnp.where(iota(BANDS)[None, :] == at[:, None], values[None, :], 0), axis=1
    )
    to = pick(lax.rem(m + iota(MD), MD), slot)
    source = pick(lax.rem(m - iota(MD) + MD, MD), jnp.where(has > 0, slot, -1))
    self = m[None]
    lane = jnp.where(iota(LANES) == pick(self, column), 1.0, 0.0)
    held = jnp.broadcast_to(pick(self, has), (LANES,)).astype(F32)
    masks = jnp.pad(jnp.stack([lane, held]), ((0, SUB - 2), (0, 0)))
    return inverse, band_owner, to, source, self, masks


def shift(part, s):
    return lax.ppermute(part, "m", [(i, (i + s) % MD) for i in range(MD)])


def shards(
    gradient, second_moment, owner_table, left_stats, right_stats, left_root, right_root, momentum
):
    inverse, band_owner, to, source, other, masks = make_plan(owner_table)
    square = (BLK, BLK)

    got = lax.all_to_all(gradient.reshape(MD, SUB, LOCAL), "m", 0, 0, tiled=True)
    new_second, tile = adam(lax.axis_index("m")[None], gradient, second_moment)
    (pay,) = call(
        spread_body,
        "svva",
        [struct(ZD, YDIM * TB + 1, SUB, LANES)],
        [inverse, tile, got, to],
        name="spread",
        prefetch=True,
        stream=True,
    )
    packed = call(
        pack_body,
        "svvva",
        [struct(3, ROW_DEV, BLK)] * MD,
        [to, left_root[0], right_root[0], momentum[0], pay],
        name="pack",
        prefetch=True,
    )
    got = lax.all_to_all(pay, "z", 0, 0, tiled=True)
    moved = {0: packed[0]}
    for s in SHIFTS:
        moved[s] = shift(packed[s], s)
    (pay,) = call(
        plane_body,
        "v" + "a" * len(SHIFTS),
        [struct(YDIM * BANDS, ZZ * TB + 1, SUB, LANES)],
        [got, *(moved[s] for s in SHIFTS)],
        name="plane",
        stream=True,
    )
    got = lax.all_to_all(pay, ("y", "m"), 0, 0, tiled=True)
    left, right, old = call(
        roots_body,
        "s" + "v" * MD,
        [struct(*square)] * 3,
        [other, *(moved[s] for s in range(MD))],
        name="roots",
    )
    whole = got
    (back,) = call(
        block_body,
        "vvvvv",
        [struct(YDIM * MD, ZZ * TB + 1, SUB, LANES)],
        [masks, whole, left, right, old],
        scratch=[
            pltpu.VMEM(square, BF16),
            pltpu.VMEM(square, BF16),
            pltpu.VMEM(square, F32),
        ],
        flops=4 * BLK**3,
        vmem=24,
        name="block",
        stream=True,
    )
    got = lax.all_to_all(back, ("y", "m"), 0, 0, tiled=True)
    parts = call(
        stats_body,
        "svv",
        [struct(3, ROW_DEV, BLK)] * MD,
        [other, whole, back],
        scratch=[pltpu.VMEM(square, BF16)] * 3,
        flops=4 * BLK**3,
        name="stats",
    )
    pay, *held = call(
        unplane_body,
        "v",
        [struct(ZD, YDIM * TB + 1, SUB, LANES)],
        [got],
        name="unplane",
        stream=True,
        hold=parts[1:],
    )
    got = lax.all_to_all(pay, "z", 0, 0, tiled=True)
    results = {0: parts[0]}
    for s in SHIFTS:
        results[s] = shift(held[s - 1], s)
    (pay,) = call(
        place_body,
        "sv" + "a" * len(SHIFTS),
        [struct(MD, SUB, LOCAL)],
        [band_owner, got, *(results[s] for s in SHIFTS)],
        name="place",
        prefetch=True,
        stream=True,
    )
    (clip,) = call(norm_body, "v", [struct(1, LANES, dtype=F32)], [got], name="norm")
    placed = lax.all_to_all(pay, "m", 0, 0, tiled=True).reshape(ROW_DEV, LOCAL)
    update = (clip[0, 0] * placed.astype(F32)).astype(BF16)
    stat = struct(SLOTS, ROW_DEV, BLK, dtype=F32)
    new_left, new_right, new_moment = call(
        finish_body,
        "svv" + "v" * MD,
        [stat, stat, struct(SLOTS, ROW_DEV, BLK)],
        [source, left_stats[0], right_stats[0], *(results[s] for s in range(MD))],
        name="finish",
    )
    return update, new_second, new_left[None], new_right[None], new_moment[None]


def solution(mesh):
    owners, groups = mesh.devices.shape
    inner = Mesh(mesh.devices.reshape(owners // YDIM, YDIM, groups), AXES)
    wide = P(("z", "y"), "m")
    stats = P(("z", "y"), None, "m", None)
    return jax.shard_map(
        shards,
        mesh=inner,
        in_specs=(wide, wide, P(), stats, stats, stats, stats, stats),
        out_specs=(wide, wide, stats, stats, stats),
        check_vma=False,
    )
```
